256 devices in a mesh: ctx: 32 (over y, x, core), head: 8 (over z).
Axes of the slice: x: 4, y: 4, z: 8, core: 2. Of those that a mesh axis runs over, the one named last changes fastest.
Arguments:
- queries: bfloat16 [16384, 2048], P('ctx', 'head'), may hold values from -50 to 50
- key_in: bfloat16 [16384, 2048], P('ctx', 'head'), may hold values from -6 to 6
- values: bfloat16 [16384, 2048], P('ctx', 'head'), may hold values from -6 to 6
- segment: int32 [16384], replicated, may hold values from 0 to 23, never falling along the last dimension, each value on 1 to 4096 neighbouring positions
- tool_ids: int32 [16384], replicated, may hold values from 0 to 256, as said below
- out_weight: bfloat16 [2048, 4096], P('head'), may hold values from -0.125 to 0.125
- grad_mixed: bfloat16 [16384, 4096], P('ctx', 'head'), may hold values from -1.5 to 1.5
Outputs:
- layer_out: bfloat16 [16384, 4096], P('ctx', 'head')
- grad_query: bfloat16 [16384, 2048], P('ctx', 'head')
- grad_key: bfloat16 [16384, 2048], P('ctx', 'head')
- grad_value: bfloat16 [16384, 2048], P('ctx', 'head')
- grad_out_weight: float32 [2048, 4096], P('head', 'ctx')
The draws below stay inside these ranges and needn't reach their ends.
Inputs may be any that keep to these rules, and one draw needn't show every extreme that they name: `segment`: document ids never fall along the sequence; every document has 1 to 4096 tokens and one has exactly 4096. `tool_ids`: tool block t > 0 is exactly the tokens 64 * (t - 1) to 64 * t - 1; tokens of no tool block carry 0.
All inputs are finite; a program needn't handle non-finite values.
Results may differ from the reference program's by a relative error of at most 0.04.
Values may be sent and summed in bfloat16 or wider, within the bound.
A program may use at most 192 MiB of HBM per device.

```python
import math
import jax
import jax.numpy as jnp
import numpy as np
from jax import lax

D = 4096
HEADS = 16
HD = 128
TOK_DEV = 512
TOOL_LEN = 64
SEQ = 16384
REACH = 8
MAXDOC = 4096
DOCS = 24


def base_keys(key):
    return jax.random.normal(key, (SEQ, HEADS * HD), jnp.float32)


def draw_key_in(key, part):
    shared = base_keys(key)
    return jnp.clip(shared, -6.0, 6.0).astype(jnp.bfloat16)


def draw_queries(key, part):
    key = jax.random.fold_in(key, 23)
    first = jax.random.fold_in(key, 0)
    own_rows = jnp.clip(jax.random.normal(first, (SEQ, HEADS * HD), jnp.float32), -6.0, 6.0)
    return own_rows.astype(jnp.bfloat16)


def draw_tool_ids(key, part):
    key = jax.random.fold_in(key, 37)
    block_total = SEQ // TOOL_LEN
    flags = jax.random.randint(key, (block_total,), 0, 4) == 0
    index = jnp.arange(block_total, dtype=jnp.int32)
    flags = (flags | (index == block_total - 1)) & (index > 0)
    block_ids = jnp.where(flags, index + 1, 0).astype(jnp.int32)
    return jnp.repeat(block_ids, TOOL_LEN, total_repeat_length=SEQ)


def with_spikes(entries, rng, source, target, shards_of, factor):
    def block_of(dim):
        return (jnp.arange(entries.shape[dim]) // (entries.shape[dim] // shards_of)).reshape((-1,) + (1,) * (entries.ndim - 1 - dim))

    first = jax.random.permutation(rng, shards_of)[block_of(target)]
    other_side = (block_of(target) + shards_of // 2) % shards_of
    return jnp.where((block_of(source) == first) | (block_of(source) == other_side), factor * entries, entries)


def shard_levels(rng, dims, cuts, smallest, high):
    def one(position, parts):
        steps = jax.random.uniform(jax.random.fold_in(jax.random.fold_in(rng, 6), position), (parts,), jnp.float32, smallest / len(cuts), high / len(cuts))
        return jnp.repeat(jnp.exp(steps), dims[position] // parts).reshape((-1,) + (1,) * (len(dims) - position - 1))

    factor_of = one(*cuts[0])
    for cut in cuts[1:]:
        factor_of = factor_of * one(*cut)
    return factor_of


def profile(count, total, bound, lean):
    portions = [(1 << 20) // math.isqrt(rank ** lean) + 1 for rank in range(2, count + 1)]
    spare, holding = total - bound - (count - 1), [1] * (count - 1)
    while spare > 0:
        free = [i for i in range(count - 1) if holding[i] < bound]
        whole, left = sum([portions[i] for i in free]), spare
        for i in free:
            extra = min(bound - holding[i], max(1, left * portions[i] // whole), spare)
            holding[i] = holding[i] + extra
            spare = spare - extra
    return np.array([bound] + holding)


def ragged(key, amount, total, limit, skew):
    if amount == 2:
        one = jax.random.randint(key, (), max(1, total - limit), min(limit, total - 1) + 1)
        return jnp.stack([one, total - one])
    tallies = jnp.asarray(profile(amount, total, limit, skew), jnp.int32)
    twos = (amount - 1) // 2
    source_of, receiver = tallies[1:1 + 2 * twos:2], tallies[2:2 + 2 * twos:2]
    room = jnp.minimum(source_of - 1, limit - receiver)
    moved = jax.random.randint(jax.random.fold_in(key, 1), (twos,), 0, 1 << 20) % (room + 1)
    tallies = tallies.at[1:1 + 2 * twos:2].set(source_of - moved).at[2:2 + 2 * twos:2].set(receiver + moved)
    return tallies[jax.random.permutation(jax.random.fold_in(key, 2), amount)]


def scatter_about(key, dims, spread, reach, shards=(), kind=jnp.bfloat16):
    entries = jax.random.normal(key, dims, jnp.float32) * spread
    if len(shards) > 0:
        entries = shard_levels(key, dims, shards, -0.22, 0.18) * entries
    return jnp.clip(entries, min=-reach, max=reach).astype(kind)


def noise_with(own_key, shape, scale, most, cuts, heavy, kind=jnp.bfloat16):
    array = scale * jax.random.normal(own_key, shape, jnp.float32)
    if cuts:
        array = array * shard_levels(own_key, shape, cuts, -0.22, 0.18)
    return jnp.clip(with_spikes(array, jax.random.fold_in(own_key, 3), *heavy), -most, most).astype(kind)


def setup_inputs(seed: int = 0) -> dict:
    key_of = jax.random.split(jax.random.key(seed), 8)
    queries = draw_queries(jax.random.fold_in(key_of[7], 71), 0)
    key_in = draw_key_in(jax.random.fold_in(key_of[7], 71), 0)
    values = scatter_about(key_of[2], (SEQ, HEADS * HD), 1.0, 6.0, ((0, 32), (1, 8)))
    segment = jnp.searchsorted(jnp.cumsum(ragged(key_of[3], DOCS, SEQ, MAXDOC, 2)), jnp.arange(SEQ), side="right").astype(jnp.int32)
    tool_ids = draw_tool_ids(jax.random.fold_in(key_of[7], 71), 0)
    out_weight = scatter_about(key_of[5], (HEADS * HD, D), (HEADS * HD) ** -0.5, 0.125, ((0, 8),))
    grad_mixed = noise_with(key_of[6], (SEQ, D), 0.25, 1.5, ((0, 32), (1, 8)), (0, 1, 32, 2.75))
    return {"queries": queries, "key_in": key_in, "values": values, "segment": segment, "tool_ids": tool_ids, "out_weight": out_weight, "grad_mixed": grad_mixed}


NEG = -1e+30

def visible(seg_query, tool_query, seg_key, tool_key, offset):
    shape_pair = (seg_query.shape[0], seg_key.shape[0])
    row_pos = lax.broadcasted_iota(jnp.int32, shape_pair, 0) + offset
    col_pos = lax.broadcasted_iota(jnp.int32, shape_pair, 1)
    same_doc = seg_query[:, None] == seg_key[None, :]
    tool_ok = (tool_key[None, :] == 0) | (tool_key[None, :] == tool_query[:, None])
    return same_doc & tool_ok & (col_pos <= row_pos)

def reference(queries, key_in, values, segment, tool_ids, out_weight, grad_mixed):
    score_scale = 1.0 / math.sqrt(HD)
    full_width = HEADS * HD
    front_rows = REACH * TOK_DEV
    window_rows = front_rows + TOK_DEV
    block_count = SEQ // TOK_DEV
    key_pad = jnp.concatenate([jnp.zeros((front_rows, full_width), key_in.dtype), key_in], axis=0)
    value_pad = jnp.concatenate([jnp.zeros((front_rows, full_width), values.dtype), values], axis=0)
    seg_pad = jnp.concatenate([jnp.full((front_rows,), -1, jnp.int32), segment.astype(jnp.int32)])
    tool_pad = jnp.concatenate([jnp.zeros((front_rows,), jnp.int32), tool_ids.astype(jnp.int32)])
    block_starts = jnp.arange(block_count, dtype=jnp.int32) * TOK_DEV

    def pieces(start_row):
        query_rows = lax.dynamic_slice_in_dim(queries, start_row, TOK_DEV, 0).astype(jnp.float32).reshape(TOK_DEV, HEADS, HD)
        key_rows = lax.dynamic_slice_in_dim(key_pad, start_row, window_rows, 0).astype(jnp.float32).reshape(window_rows, HEADS, HD)
        value_rows = lax.dynamic_slice_in_dim(value_pad, start_row, window_rows, 0).astype(jnp.float32).reshape(window_rows, HEADS, HD)
        visible_now = visible(lax.dynamic_slice_in_dim(segment, start_row, TOK_DEV, 0), lax.dynamic_slice_in_dim(tool_ids, start_row, TOK_DEV, 0), lax.dynamic_slice_in_dim(seg_pad, start_row, window_rows, 0), lax.dynamic_slice_in_dim(tool_pad, start_row, window_rows, 0), front_rows)
        scores = jnp.einsum('thd,khd->htk', query_rows, key_rows) * score_scale
        scores = jnp.where(visible_now[None], scores, NEG)
        top_score = lax.optimization_barrier(jnp.max(scores, axis=2, keepdims=True))
        log_total = top_score + jnp.log(lax.optimization_barrier(jnp.sum(jnp.exp(scores - top_score), axis=2, keepdims=True)))
        probs = jnp.where(visible_now[None], jnp.exp(scores - log_total), 0.0)
        return (query_rows, key_rows, value_rows, probs)

    def forward_block(start_row):
        query_rows, key_rows, value_rows, probs = pieces(start_row)
        probs_low = lax.optimization_barrier(probs.astype(jnp.bfloat16)).astype(jnp.float32)
        return jnp.einsum('htk,khd->thd', probs_low, value_rows).reshape(TOK_DEV, full_width).astype(jnp.bfloat16)
    attended = lax.map(forward_block, block_starts).reshape(SEQ, full_width)
    layer_out = jnp.dot(attended, out_weight, preferred_element_type=jnp.float32).astype(jnp.bfloat16)
    grad_attended = jnp.dot(grad_mixed, out_weight.T, preferred_element_type=jnp.float32).astype(jnp.bfloat16)
    grad_out_weight = jnp.dot(attended.T, grad_mixed, preferred_element_type=jnp.float32)

    def backward_block(accums, start_row):
        key_acc, value_acc = accums
        query_rows, key_rows, value_rows, probs = pieces(start_row)
        probs_low = lax.optimization_barrier(probs.astype(jnp.bfloat16)).astype(jnp.float32)
        grad_rows = lax.dynamic_slice_in_dim(grad_attended, start_row, TOK_DEV, 0).astype(jnp.float32).reshape(TOK_DEV, HEADS, HD)
        attended_rows = lax.dynamic_slice_in_dim(attended, start_row, TOK_DEV, 0).astype(jnp.float32).reshape(TOK_DEV, HEADS, HD)
        row_delta = lax.optimization_barrier(jnp.sum(grad_rows * attended_rows, axis=2)).T
        grad_probs = jnp.einsum('thd,khd->htk', grad_rows, value_rows)
        grad_scores = probs * (grad_probs - row_delta[:, :, None]) * score_scale
        grad_scores = lax.optimization_barrier(grad_scores.astype(jnp.bfloat16)).astype(jnp.float32)
        query_grad = jnp.einsum('htk,khd->thd', grad_scores, key_rows).reshape(TOK_DEV, full_width).astype(jnp.bfloat16)
        key_part = jnp.einsum('htk,thd->khd', grad_scores, query_rows).reshape(window_rows, full_width)
        value_part = jnp.einsum('htk,thd->khd', probs_low, grad_rows).reshape(window_rows, full_width)
        key_acc = lax.dynamic_update_slice_in_dim(key_acc, lax.dynamic_slice_in_dim(key_acc, start_row, window_rows, 0) + key_part, start_row, 0)
        value_acc = lax.dynamic_update_slice_in_dim(value_acc, lax.dynamic_slice_in_dim(value_acc, start_row, window_rows, 0) + value_part, start_row, 0)
        return ((key_acc, value_acc), query_grad)
    zeros_full = jnp.zeros((front_rows + SEQ, full_width), jnp.float32)
    (key_acc, value_acc), grad_query = lax.scan(backward_block, (zeros_full, zeros_full), block_starts)
    grad_query = grad_query.reshape(SEQ, full_width)
    grad_key = key_acc[front_rows:].astype(jnp.bfloat16)
    grad_value = value_acc[front_rows:].astype(jnp.bfloat16)
    return (layer_out, grad_query, grad_key, grad_value, grad_out_weight)
```

```python
import functools
import math

import jax
import jax.numpy as jnp
from jax import lax
from jax.experimental import pallas as pl
from jax.experimental.pallas import tpu as pltpu
from jax.sharding import PartitionSpec as P

HD = 128
T = 512
CT = 1024
SUB = 256
REACH = 4
DOCS = 24
TOOLS = 16
LSE_ROW = DOCS + TOOLS
MASK = 131072.0
SCALE = 1.0 / math.sqrt(HD)
LOG2 = SCALE * math.log2(math.e)
MESH = pl.DeviceIdType.MESH
F32 = jnp.float32
BF16 = jnp.bfloat16


def dot(a, b):
    return jnp.dot(a, b, preferred_element_type=F32)


def dot_tn(a, b):
    return lax.dot_general(a, b, (((0,), (0,)), ((), ())), preferred_element_type=F32)


def dot_nt(a, b):
    return lax.dot_general(a, b, (((1,), (1,)), ((), ())), preferred_element_type=F32)


def thirds(x):
    high = x.astype(BF16)
    rest = x - high.astype(F32)
    mid = rest.astype(BF16)
    return high.astype(F32), mid.astype(F32), (rest - mid.astype(F32))


def kernel(
    nc, nz,
    seg, tool, q_in, k_in, v_in, w_in, gm_in,
    out, dq_out, dk_out, dv_out, gw_out,
    qs, kv, fk, qt, m_s, l_s, ot, otb, ob, gmf, da, dos, dob, dotr, dqt, wsl, atf, lo,
    d0, sa, sb, s4, ra, rb, rf, rf4, fin, pg, gown, gws, gwr, gsum, gwi,
    swap_s, swap_r, kv_s, kv_r, zg_s, zg_r, za_s, za_r, w1_s, w1_r, w2_s, w2_r,
    w3_s, w3_r, at_s, at_r, do_s, do_r, ch_s, ch_r, fn_s, fn_r, gx_s, gx_r, gw_s, gw_r,
):
    me = lax.axis_index("ctx")
    z = lax.axis_index("head")
    m = me // 2
    c = lax.rem(me, 2)
    o = 1 - c
    sib = me + 1 - 2 * c

    def chip(by):
        return lax.rem(m + by + nc, nc)

    def at_chip(by):
        return 2 * chip(by) + c

    def zed(by):
        return lax.rem(z + by + nz, nz)

    def remote(src, dst, ss, rs, ctx, head):
        return pltpu.make_async_remote_copy(
            src_ref=src, dst_ref=dst, send_sem=ss, recv_sem=rs,
            device_id=(ctx, head), device_id_type=MESH,
        )

    def cols(index, width):
        return pl.ds(pl.multiple_of(index * width, width), width)

    sent = []

    def start(copy):
        copy.start()
        sent.append(copy)

    barrier = pltpu.get_barrier_semaphore()
    pl.semaphore_signal(barrier, inc=1, device_id=(sib, z), device_id_type=MESH)

    @pl.loop(1, nc)
    def _(by):
        pl.semaphore_signal(barrier, inc=1, device_id=(at_chip(by), z), device_id_type=MESH)

    @pl.loop(1, nz)
    def _(by):
        pl.semaphore_signal(barrier, inc=1, device_id=(me, zed(by)), device_id_type=MESH)

    pl.semaphore_wait(barrier, 1 + (nc - 1) + (nz - 1))

    for t, (src, dst) in enumerate(((q_in, qs.at[c]), (k_in, kv.at[0, c, 0]), (v_in, kv.at[0, c, 1]))):
        start(remote(src.at[:, cols(o, HD)], dst, swap_s.at[t], swap_r.at[t], sib, z))

    full = nz // 2 - 1

    def ring_has(step, half, right):
        return step <= full or (step == full + 1 and half == (0 if right else 1))

    def ring_send(buf, ss, rs, step, half, src=None):
        for side, right in enumerate((True, False)):
            if ring_has(step, half, right):
                block = zed(1 - step) if right else zed(step - 1)
                to = zed(1) if right else zed(-1)
                k = side * 8 + (step - 1) * 2 + half
                dst = buf.at[block, half]
                start(remote(dst if src is None else src, dst, ss.at[k], rs.at[k], me, to))

    def ring_recv(buf, ss, rs, step, half):
        for side, right in enumerate((True, False)):
            if ring_has(step, half, right):
                block = zed(-step) if right else zed(step)
                k = side * 8 + (step - 1) * 2 + half
                dst = buf.at[block, half]
                remote(dst, dst, ss.at[k], rs.at[k], me, z).wait_recv()

    for half in range(2):
        ring_send(gmf, zg_s, zg_r, 1, half, gm_in.at[half])

    rows16 = pl.ds(pl.multiple_of(m * 16, 16), 16)
    wide = cols(c, SUB)

    @pl.loop(1, nz)
    def _(by):
        to = zed(by)
        src = w_in.at[rows16, pl.ds(pl.multiple_of(to * T + c * SUB, SUB), SUB)]
        remote(src, wsl.at[z, rows16, wide], w1_s.at[by], w1_r.at[by], me, to).start()

    wsl[z, rows16, wide] = w_in[rows16, pl.ds(pl.multiple_of(z * T + c * SUB, SUB), SUB)]

    gmf[z] = gm_in[...]
    qs[c] = q_in[:, cols(c, HD)]
    kv[0, c, 0] = k_in[:, cols(c, HD)]
    kv[0, c, 1] = v_in[:, cols(c, HD)]

    row = lax.broadcasted_iota(jnp.int32, (HD, CT), 0)
    pos = lax.broadcasted_iota(jnp.int32, (HD, CT), 1)
    block64 = lax.shift_right_logical(pos, 6)
    is_doc = row < DOCS
    is_tool = (row >= DOCS) & (row < LSE_ROW)
    for d in range(REACH + 1):
        seg_row = seg[pl.ds(chip(-d), 1), :]
        tool_row = tool[pl.ds(chip(-d), 1), :]
        if d == 0:
            bad_tool = (block64 > row - DOCS) | ((tool_row != 0) & (block64 != row - DOCS))
        else:
            bad_tool = jnp.broadcast_to(tool_row != 0, row.shape)
        bad = (is_doc & (seg_row != row)) | (is_tool & bad_tool)
        feat = jnp.where(bad, -MASK, jnp.where((row >= LSE_ROW) & (row < LSE_ROW + 3), -1.0, 0.0))
        fk[d] = feat.T.astype(BF16)
    seg_row = seg[pl.ds(m, 1), :]
    hot = (is_doc & (seg_row == row)) | (is_tool & (block64 == row - DOCS))
    qfeat = jnp.where(hot, 1.0, 0.0)
    qt[HD:, :] = qfeat.astype(BF16)

    for t, dst in enumerate((qs.at[o], kv.at[0, o, 0], kv.at[0, o, 1])):
        remote(dst, dst, swap_s.at[t], swap_r.at[t], sib, z).wait_recv()

    kv_moves = {
        (1, 0): (0, 1), (3, 1): (0, 3), (4, 0): (0, 4), (4, 1): (0, 4),
        (2, 0): (1, 1), (3, 0): (2, 1), (2, 1): (3, -1), (1, 1): (2, -1),
    }
    kv_key = {key: index for index, key in enumerate(kv_moves)}

    def kv_send(key):
        source, by = kv_moves[key]
        k = kv_key[key]
        start(remote(kv.at[source, key[1]], kv.at[key], kv_s.at[k], kv_r.at[k], at_chip(by), z))

    def kv_recv(key):
        k = kv_key[key]
        remote(kv.at[key], kv.at[key], kv_s.at[k], kv_r.at[k], me, z).wait_recv()

    for key in ((1, 0), (3, 1), (4, 0), (4, 1)):
        kv_send(key)

    qt[:HD, :] = jnp.concatenate([qs[0].astype(F32).T, qs[1].astype(F32).T], axis=1).astype(BF16)
    m_s[...] = jnp.full(m_s.shape, -1e30, F32)
    l_s[...] = jnp.zeros(l_s.shape, F32)
    ot[...] = jnp.zeros(ot.shape, F32)
    da[...] = jnp.zeros(da.shape, F32)

    def span(key):
        if key == (0, 1):
            return T, T
        if key == (REACH, 0):
            return 0, T
        return 0, CT

    def scores(key, sub):
        d, h = key
        q0, qn = span(key)
        rows = pl.ds(pl.multiple_of(sub * SUB, SUB), SUB)
        frows = pl.ds(pl.multiple_of(h * T + sub * SUB, SUB), SUB)
        k_tile = kv[d, h, 0, rows, :]
        s = dot(jnp.concatenate([k_tile, fk[d, frows, :]], axis=1), qt[:, q0:q0 + qn])
        if d == 0:
            key_pos = h * T + sub * SUB + lax.broadcasted_iota(jnp.int32, s.shape, 0)
            query_pos = q0 + lax.broadcasted_iota(jnp.int32, s.shape, 1)
            s = jnp.where(key_pos <= query_pos, s, -2.0 * MASK)
        return s, k_tile, kv[d, h, 1, rows, :]

    def forward(key):
        q0, qn = span(key)

        @pl.loop(0, T // SUB)
        def _(sub):
            s, _, v_tile = scores(key, sub)
            old = m_s[:, q0:q0 + qn]
            new = jnp.maximum(old, jnp.max(s, axis=0, keepdims=True))
            p = jnp.exp2((s - new) * LOG2)
            fade = jnp.exp2((old - new) * LOG2)
            m_s[:, q0:q0 + qn] = new
            l_s[:, q0:q0 + qn] = l_s[:, q0:q0 + qn] * fade + jnp.sum(p, axis=0, keepdims=True)
            ot[:, q0:q0 + qn] = ot[:, q0:q0 + qn] * fade + dot_tn(v_tile, p.astype(BF16))

    def grad_block(block):
        w_cols = w_in[:, pl.ds(pl.multiple_of(block * T, T), T)]
        for half in range(2):
            rows = slice(half * SUB, half * SUB + SUB)
            da[rows, :] = da[rows, :] + dot_nt(gmf[block, half], w_cols)

    def gm_step(k):
        step, half = k // 2 + 1, k % 2
        ring_recv(gmf, zg_s, zg_r, step, half)
        ring_send(gmf, zg_s, zg_r, step + 1, half)

    def kv_step(key, then=None):
        kv_recv(key)
        if then is not None:
            kv_send(then)

    forward((0, 0))
    forward((0, 1))
    kv_step((1, 0), (2, 0))
    gm_step(0)
    forward((1, 0))
    kv_step((3, 1), (2, 1))
    grad_block(z)
    forward((3, 1))
    kv_step((2, 0), (3, 0))
    gm_step(1)
    forward((2, 0))
    kv_step((2, 1), (1, 1))
    forward((2, 1))
    kv_recv((4, 0))
    forward((4, 0))
    grad_block(zed(1))
    grad_block(zed(-1))
    gm_step(2)
    kv_recv((3, 0))
    forward((3, 0))
    kv_recv((4, 1))
    forward((4, 1))

    @pl.loop(1, nz)
    def _(by):
        src = wsl.at[zed(-by), rows16, wide]
        remote(src, src, w1_s.at[by], w1_r.at[by], me, z).wait_recv()

    gm_step(3)
    kv_recv((1, 1))
    forward((1, 1))

    @pl.loop(1, nc)
    def _(by):
        src = wsl.at[:, rows16, wide]
        remote(src, src, w2_s.at[by], w2_r.at[by], at_chip(by), z).start()

    inv = 1.0 / l_s[...]
    lse = m_s[...] + jnp.log2(l_s[...]) * (1.0 / LOG2)
    att = ot[...] * inv
    otb[...] = att.astype(BF16)
    for h in range(2):
        ob[h] = att[:, h * T:(h + 1) * T].T.astype(BF16).reshape(2, SUB, HD)
    mine = cols(c, HD)
    start(remote(ob.at[o], atf.at[z, :, :, mine], at_s, at_r, sib, z))
    atf[z, :, :, mine] = ob[c]
    high, mid, low = thirds(lse)
    qt[HD:, :] = jnp.where(
        row == LSE_ROW, high,
        jnp.where(row == LSE_ROW + 1, mid, jnp.where(row == LSE_ROW + 2, low, qfeat)),
    ).astype(BF16)
    dst = atf.at[z, :, :, cols(o, HD)]
    remote(dst, dst, at_s, at_r, sib, z).wait_recv()

    def weight_block(block):
        part = dot_tn(atf[z, 0], gmf[block, 0]) + dot_tn(atf[z, 1], gmf[block, 1])
        pg[...] = part
        per = nc // nz
        for e in range(per):
            gown[block * per + e] = pg[:, pl.ds(pl.multiple_of(e * SUB + c * HD, HD), HD)]
            gws[block * per + e] = pg[:, pl.ds(pl.multiple_of(e * SUB + o * HD, HD), HD)].astype(BF16)

    grad_block(zed(2))
    grad_block(zed(-2))
    for by in (0, 1, -1, 2, -2):
        weight_block(zed(by))
    gm_step(4)
    gm_step(5)
    for half in range(2):
        ring_send(atf, za_s, za_r, 1, half)
    for by in (3, -3):
        grad_block(zed(by))
        weight_block(zed(by))
    gm_step(6)
    gm_step(7)
    grad_block(zed(4))

    dos[...] = da[:, cols(o, HD)].astype(BF16)
    start(remote(dos, dob.at[c], do_s, do_r, sib, z))
    dob[c] = da[:, mine].astype(BF16)

    weight_block(zed(4))
    start(remote(gws, gwr, gx_s, gx_r, sib, z))

    remote(dob.at[o], dob.at[o], do_s, do_r, sib, z).wait_recv()
    dot_rows = jnp.concatenate([dob[0].astype(F32).T, dob[1].astype(F32).T], axis=1)
    dotr[:HD, :] = dot_rows.astype(BF16)
    delta = jnp.sum(dot_rows * otb[...].astype(F32), axis=0, keepdims=True)
    high, mid, low = thirds(delta)
    dotr[HD:, :] = jnp.where(
        row == 0, high, jnp.where(row == 1, mid, jnp.where(row == 2, low, 0.0))
    ).astype(BF16)
    dqt[...] = jnp.zeros(dqt.shape, F32)
    minus = jnp.where(lax.broadcasted_iota(jnp.int32, (SUB, HD), 1) < 3, -1.0, 0.0).astype(BF16)

    def backward(key, finish):
        q0, qn = span(key)

        @pl.loop(0, T // SUB)
        def _(sub):
            rows = pl.ds(pl.multiple_of(sub * SUB, SUB), SUB)
            s, k_tile, v_tile = scores(key, sub)
            p = jnp.exp2(s * LOG2)
            dp = dot(jnp.concatenate([v_tile, minus], axis=1), dotr[:, q0:q0 + qn])
            ds = (p * dp).astype(BF16)
            if qn == CT:
                do_rows = dob[...].reshape(CT, HD)
                q_rows = qs[...].reshape(CT, HD)
            else:
                do_rows = dob[q0 // T]
                q_rows = qs[q0 // T]
            finish(rows, dot(ds, q_rows) * SCALE, dot(p.astype(BF16), do_rows))
            dqt[:, q0:q0 + qn] = dqt[:, q0:q0 + qn] + dot_tn(k_tile, ds)

    def keep(buf, *slot):
        def finish(rows, dk, dv):
            buf[(*slot, 0, rows)] = dk.astype(buf.dtype)
            buf[(*slot, 1, rows)] = dv.astype(buf.dtype)
        return finish

    def add_keep(buf, other, *slot):
        def finish(rows, dk, dv):
            buf[(*slot, 0, rows)] = (dk + other[(*slot, 0, rows)].astype(F32)).astype(BF16)
            buf[(*slot, 1, rows)] = (dv + other[(*slot, 1, rows)].astype(F32)).astype(BF16)
        return finish

    def att_step(k):
        step, half = k // 2 + 1, k % 2
        ring_recv(atf, za_s, za_r, step, half)
        ring_send(atf, za_s, za_r, step + 1, half)

    def stage(s):
        a, b = (s, 0), (REACH - s, 1)
        if s == 1:
            backward(a, keep(sa, 0))
        else:
            remote(ra.at[s - 1], ra.at[s - 1], ch_s.at[s - 2], ch_r.at[s - 2], me, z).wait_recv()
            backward(a, add_keep(sa, ra, s - 1))
        if s < REACH - 1:
            start(remote(sa.at[s - 1], ra.at[s], ch_s.at[s - 1], ch_r.at[s - 1], at_chip(1), z))
        else:
            start(remote(sa.at[s - 1], rf.at[0], ch_s.at[s - 1], ch_r.at[s - 1], at_chip(-3), z))
        if s == 1:
            backward(b, keep(sb, 0))
        else:
            remote(rb.at[s - 1], rb.at[s - 1], ch_s.at[s + 1], ch_r.at[s + 1], me, z).wait_recv()
            backward(b, add_keep(sb, rb, s - 1))
        if s < REACH - 1:
            start(remote(sb.at[s - 1], rb.at[s], ch_s.at[s + 2], ch_r.at[s + 2], at_chip(-1), z))
        else:
            start(remote(sb.at[s - 1], rf.at[1], ch_s.at[s + 2], ch_r.at[s + 2], at_chip(-1), z))

    stage(1)
    att_step(0)

    remote(gwr, gwr, gx_s, gx_r, sib, z).wait_recv()

    @pl.loop(1, nc)
    def _(by):
        to = lax.rem(m + by, nc)
        gsum[to] = (gown[to] + gwr[to].astype(F32)).astype(BF16)
        remote(gsum.at[to], gwi.at[by], gw_s.at[by], gw_r.at[by], at_chip(by), z).start()

    att_step(1)
    for h in range(2):
        backward((REACH, h), keep(s4, h))
    start(remote(s4, rf4, ch_s.at[6], ch_r.at[6], at_chip(-4), z))
    att_step(2)
    stage(2)
    att_step(3)
    for h in range(2):
        backward((0, h), keep(d0, h))

    @pl.loop(1, nc)
    def _(by):
        src = wsl.at[:, pl.ds(pl.multiple_of(chip(-by) * 16, 16), 16), wide]
        remote(src, src, w2_s.at[by], w2_r.at[by], me, z).wait_recv()

    start(remote(wsl.at[:, :, wide], wsl.at[:, :, wide], w3_s, w3_r, sib, z))
    att_step(4)
    att_step(5)
    stage(3)

    fin[0, 0] = (dqt[:, :T] * SCALE).T.astype(BF16)
    fin[0, 1] = (dqt[:, T:] * SCALE).T.astype(BF16)
    outs = (dq_out, dk_out, dv_out)
    start(remote(fin.at[0, o], dq_out.at[:, mine], fn_s.at[0], fn_r.at[0], sib, z))
    dq_out[:, mine] = fin[0, c]

    other = wsl.at[:, :, cols(o, SUB)]
    remote(other, other, w3_s, w3_r, sib, z).wait_recv()

    def out_block(block, first=False):
        for half in range(2):
            rows = slice(half * SUB, half * SUB + SUB)
            part = dot(atf[block, half], wsl[block])
            lo[rows, :] = part if first else lo[rows, :] + part

    out_block(z, True)
    for by in (1, -1, 2, -2, 3, -3):
        out_block(zed(by))

    total = gown[m] + gwr[m].astype(F32)
    for by in range(1, nc):
        remote(gwi.at[by], gwi.at[by], gw_s.at[by], gw_r.at[by], me, z).wait_recv()
        total = total + gwi[by].astype(F32)
    gw_out[...] = total

    att_step(6)
    att_step(7)
    out_block(zed(4))
    out[...] = lo[...].astype(BF16)

    remote(rf4, rf4, ch_s.at[6], ch_r.at[6], me, z).wait_recv()
    for h in range(2):
        remote(rf.at[h], rf.at[h], ch_s.at[2 + 3 * h], ch_r.at[2 + 3 * h], me, z).wait_recv()
        for t in range(2):
            fin[1 + t, h] = (d0[h, t] + rf[h, t].astype(F32) + rf4[h, t].astype(F32)).astype(BF16)
    for t in (1, 2):
        start(remote(fin.at[t, o], outs[t].at[:, mine], fn_s.at[t], fn_r.at[t], sib, z))
        outs[t][:, mine] = fin[t, c]
    for t in range(3):
        dst = outs[t].at[:, cols(o, HD)]
        remote(dst, dst, fn_s.at[t], fn_r.at[t], sib, z).wait_recv()

    for copy in sent:
        copy.wait_send()

    @pl.loop(1, nz)
    def _(by):
        src = wsl.at[z, rows16, wide]
        remote(src, src, w1_s.at[by], w1_r.at[by], me, zed(by)).wait_send()

    @pl.loop(1, nc)
    def _(by):
        src = wsl.at[:, rows16, wide]
        remote(src, src, w2_s.at[by], w2_r.at[by], at_chip(by), z).wait_send()
        remote(gwi.at[by], gwi.at[by], gw_s.at[by], gw_r.at[by], at_chip(by), z).wait_send()


def body(nc, nz, queries, key_in, values, segment, tool_ids, out_weight, grad_mixed):
    width = out_weight.shape[1]
    vm = pltpu.VMEM
    dma = pltpu.SemaphoreType.DMA
    one = dma(())
    grads = (2, T, HD)
    scratch = [
        vm((2, T, HD), BF16),
        vm((REACH + 1, 2, 2, T, HD), BF16),
        vm((REACH + 1, CT, HD), BF16),
        vm((2 * HD, CT), BF16),
        vm((1, CT), F32), vm((1, CT), F32),
        vm((HD, CT), F32),
        vm((HD, CT), BF16),
        vm((2, 2, SUB, HD), BF16),
        vm((nz, 2, SUB, T), BF16),
        vm((T, 2 * HD), F32),
        vm((T, HD), BF16),
        vm((2, T, HD), BF16),
        vm((2 * HD, CT), BF16),
        vm((HD, CT), F32),
        vm((nz, 2 * HD, T), BF16),
        vm((nz, 2, SUB, 2 * HD), BF16),
        vm((T, T), F32),
        vm((2, *grads), F32),
        vm((3, *grads), BF16), vm((3, *grads), BF16),
        vm((2, *grads), BF16),
        vm((3, *grads), BF16), vm((3, *grads), BF16),
        vm((2, *grads), BF16), vm((2, *grads), BF16),
        vm((3, 2, T, HD), BF16),
        vm((2 * HD, T), F32),
        vm((nc, 2 * HD, HD), F32),
        vm((nc, 2 * HD, HD), BF16), vm((nc, 2 * HD, HD), BF16),
        vm((nc, 2 * HD, HD), BF16), vm((nc, 2 * HD, HD), BF16),
        dma((3,)), dma((3,)),
        dma((8,)), dma((8,)),
        dma((16,)), dma((16,)), dma((16,)), dma((16,)),
        dma((nz,)), dma((nz,)), dma((nc,)), dma((nc,)), one, one,
        one, one, one, one,
        dma((7,)), dma((7,)), dma((3,)), dma((3,)),
        one, one, dma((nc,)), dma((nc,)),
    ]
    return pl.pallas_call(
        functools.partial(kernel, nc, nz),
        out_shape=(
            jax.ShapeDtypeStruct((T, width // nz), BF16),
            jax.ShapeDtypeStruct(queries.shape, BF16),
            jax.ShapeDtypeStruct(queries.shape, BF16),
            jax.ShapeDtypeStruct(queries.shape, BF16),
            jax.ShapeDtypeStruct((2 * HD, width // (2 * nc)), F32),
        ),
        in_specs=[pl.BlockSpec(memory_space=pltpu.VMEM)] * 7,
        out_specs=[pl.BlockSpec(memory_space=pltpu.VMEM)] * 5,
        scratch_shapes=scratch,
        compiler_params=pltpu.CompilerParams(
            collective_id=0, has_side_effects=True, vmem_limit_bytes=58 * 1024 * 1024
        ),
        cost_estimate=pl.CostEstimate(
            flops=20_000_000_000, bytes_accessed=8_000_000, transcendentals=10_000_000
        ),
    )(
        segment.reshape(nc, CT), tool_ids.reshape(nc, CT),
        queries, key_in, values, out_weight, grad_mixed.reshape(2, SUB, width // nz),
    )


def solution(mesh):
    nc, nz = mesh.shape["ctx"] // 2, mesh.shape["head"]
    split = P("ctx", "head")
    return jax.shard_map(
        functools.partial(body, nc, nz),
        mesh=mesh,
        in_specs=(split, split, split, P(), P(), P("head", None), split),
        out_specs=(split, split, split, split, P("head", "ctx")),
        check_vma=False,
    )
```

```python
import functools
import math

import jax
import jax.numpy as jnp
from jax import lax
from jax.experimental import pallas as pl
from jax.experimental.pallas import tpu as pltpu
from jax.sharding import PartitionSpec as P

HD = 128
T = 512
CT = 1024
SUB = 256
NX = 4
REACH = 4
DOCS = 24
TOOLS = 16
LSE_ROW = DOCS + TOOLS
MASK = 131072.0
SCALE = 1.0 / math.sqrt(HD)
LOG2 = SCALE * math.log2(math.e)
MESH = pl.DeviceIdType.MESH
F32 = jnp.float32
BF16 = jnp.bfloat16


def dot(a, b):
    return jnp.dot(a, b, preferred_element_type=F32)


def dot_tn(a, b):
    return lax.dot_general(a, b, (((0,), (0,)), ((), ())), preferred_element_type=F32)


def dot_nt(a, b):
    return lax.dot_general(a, b, (((1,), (1,)), ((), ())), preferred_element_type=F32)


def thirds(x):
    high = x.astype(BF16)
    rest = x - high.astype(F32)
    mid = rest.astype(BF16)
    return high.astype(F32), mid.astype(F32), (rest - mid.astype(F32))


def kernel(
    nc, nz,
    seg, tool, q_in, k_in, v_in, w_in, gm_in,
    out, dq_out, dk_out, dv_out, gw_out,
    qs, kv, fk, qt, m_s, l_s, ot, otb, ob, gmf, da, dos, dob, dotr, dqt, wsl, atf, lo,
    acc, snd, r1, r2, r3, fin, pg, gown, gws, gwr, ysend, yin, xown, xsend, xin,
    swap_s, swap_r, kv_s, kv_r, zg_s, zg_r, za_s, za_r, w1_s, w1_r, wx_s, wx_r, wy_s, wy_r,
    w3_s, w3_r, at_s, at_r, do_s, do_r, c1_s, c1_r, c2_s, c2_r, c3_s, c3_r,
    fn_s, fn_r, gx_s, gx_r, gy_s, gy_r, gt_s, gt_r,
):
    me = lax.axis_index("ctx")
    z = lax.axis_index("head")
    m = me // 2
    c = lax.rem(me, 2)
    o = 1 - c
    sib = me + 1 - 2 * c

    ny = nc // NX
    y = m // NX
    x = lax.rem(m, NX)

    def chip(by):
        return lax.rem(m + by + nc, nc)

    def mate(dy, dx):
        return 2 * (lax.rem(y + dy + ny, ny) * NX + lax.rem(x + dx + NX, NX)) + c

    def zed(by):
        return lax.rem(z + by + nz, nz)

    def remote(src, dst, ss, rs, ctx, head):
        return pltpu.make_async_remote_copy(
            src_ref=src, dst_ref=dst, send_sem=ss, recv_sem=rs,
            device_id=(ctx, head), device_id_type=MESH,
        )

    def cols(index, width):
        return pl.ds(pl.multiple_of(index * width, width), width)

    sent = []

    def start(copy):
        copy.start()
        sent.append(copy)

    barrier = pltpu.get_barrier_semaphore()
    pl.semaphore_signal(barrier, inc=1, device_id=(sib, z), device_id_type=MESH)

    for by in range(1, NX):
        pl.semaphore_signal(barrier, inc=1, device_id=(mate(0, by), z), device_id_type=MESH)
    for by in range(1, ny):
        pl.semaphore_signal(barrier, inc=1, device_id=(mate(by, 0), z), device_id_type=MESH)

    @pl.loop(1, nz)
    def _(by):
        pl.semaphore_signal(barrier, inc=1, device_id=(me, zed(by)), device_id_type=MESH)

    pl.semaphore_wait(barrier, 1 + (NX - 1) + (ny - 1) + (nz - 1))

    for t, (src, dst) in enumerate(((q_in, qs.at[c]), (k_in, kv.at[0, c, 0]), (v_in, kv.at[0, c, 1]))):
        start(remote(src.at[:, cols(o, HD)], dst, swap_s.at[t], swap_r.at[t], sib, z))

    full = nz // 2 - 1

    def ring_has(step, half, right):
        return step <= full or (step == full + 1 and half == (0 if right else 1))

    def ring_send(buf, ss, rs, step, half, src=None):
        for side, right in enumerate((True, False)):
            if ring_has(step, half, right):
                block = zed(1 - step) if right else zed(step - 1)
                to = zed(1) if right else zed(-1)
                k = side * 8 + (step - 1) * 2 + half
                dst = buf.at[block, half]
                start(remote(dst if src is None else src, dst, ss.at[k], rs.at[k], me, to))

    def ring_recv(buf, ss, rs, step, half):
        for side, right in enumerate((True, False)):
            if ring_has(step, half, right):
                block = zed(-step) if right else zed(step)
                k = side * 8 + (step - 1) * 2 + half
                dst = buf.at[block, half]
                remote(dst, dst, ss.at[k], rs.at[k], me, z).wait_recv()

    for half in range(2):
        ring_send(gmf, zg_s, zg_r, 1, half, gm_in.at[half])

    rows16 = pl.ds(pl.multiple_of(m * 16, 16), 16)
    wide = cols(c, SUB)

    @pl.loop(1, nz)
    def _(by):
        to = zed(by)
        src = w_in.at[rows16, pl.ds(pl.multiple_of(to * T + c * SUB, SUB), SUB)]
        remote(src, wsl.at[z, rows16, wide], w1_s.at[by], w1_r.at[by], me, to).start()

    wsl[z, rows16, wide] = w_in[rows16, pl.ds(pl.multiple_of(z * T + c * SUB, SUB), SUB)]

    gmf[z] = gm_in[...]
    qs[c] = q_in[:, cols(c, HD)]
    kv[0, c, 0] = k_in[:, cols(c, HD)]
    kv[0, c, 1] = v_in[:, cols(c, HD)]

    for t, dst in enumerate((qs.at[o], kv.at[0, o, 0], kv.at[0, o, 1])):
        remote(dst, dst, swap_s.at[t], swap_r.at[t], sib, z).wait_recv()

    inner = (x == 1) | (x == 2)

    def kv_copy(slot, h):
        if slot == 1:
            src, to = jnp.where(x < NX - 1, 0, REACH), mate(0, 1)
        elif slot == 3:
            src, to = jnp.where(x > 0, REACH, 0), mate(0, -1)
        else:
            src, to = 0, mate(1, 0)
        return remote(kv.at[src, h], kv.at[slot, h], kv_s.at[slot, h], kv_r.at[slot, h], to, z)

    def kv_on(side, h):
        src, to = ((1, mate(0, 1)), (3, mate(0, -1)))[side]
        return remote(kv.at[src, h], kv.at[2, h], kv_s.at[5 + side, h], kv_r.at[2, h], to, z)

    def kv_recv(slot, h):
        remote(kv.at[slot, h], kv.at[slot, h], kv_s.at[slot, h], kv_r.at[slot, h], me, z).wait_recv()

    def kv_forward(slot, h):
        kv_recv(slot, h)
        if slot == REACH:
            pl.when(x == NX - 1)(kv_copy(1, h).start)
            pl.when(x > 0)(kv_copy(3, h).start)
        else:
            pl.when(inner)(kv_on(slot // 2, h).start)

    for h in range(2):
        kv_copy(REACH, h).start()
        pl.when(x < NX - 1)(kv_copy(1, h).start)
        pl.when(x == 0)(kv_copy(3, h).start)

    def ids(ref, index):
        rows = ref[pl.ds(pl.multiple_of(index * 8, 8), 8), :]
        return jnp.concatenate([rows[r:r + 1, :] for r in range(8)], axis=1)

    row = lax.broadcasted_iota(jnp.int32, (HD, CT), 0)
    pos = lax.broadcasted_iota(jnp.int32, (HD, CT), 1)
    block64 = lax.shift_right_logical(pos, 6)
    is_doc = row < DOCS
    is_tool = (row >= DOCS) & (row < LSE_ROW)
    for d in range(REACH + 1):
        seg_row, tool_row = ids(seg, chip(-d)), ids(tool, chip(-d))
        if d == 0:
            bad_tool = (block64 > row - DOCS) | ((tool_row != 0) & (block64 != row - DOCS))
        else:
            bad_tool = jnp.broadcast_to(tool_row != 0, row.shape)
        bad = (is_doc & (seg_row != row)) | (is_tool & bad_tool)
        feat = jnp.where(bad, -MASK, jnp.where((row >= LSE_ROW) & (row < LSE_ROW + 3), -1.0, 0.0))
        fk[d] = feat.T.astype(BF16)
    seg_row = ids(seg, m)
    hot = (is_doc & (seg_row == row)) | (is_tool & (block64 == row - DOCS))
    qfeat = jnp.where(hot, 1.0, 0.0)
    qt[HD:, :] = qfeat.astype(BF16)

    qt[:HD, :] = jnp.concatenate([qs[0].astype(F32).T, qs[1].astype(F32).T], axis=1).astype(BF16)
    m_s[...] = jnp.full(m_s.shape, -1e30, F32)
    l_s[...] = jnp.zeros(l_s.shape, F32)
    ot[...] = jnp.zeros(ot.shape, F32)
    da[...] = jnp.zeros(da.shape, F32)

    def span(key):
        if key == (0, 1):
            return T, T
        if key == (REACH, 0):
            return 0, T
        return 0, CT

    def scores(key, sub):
        d, h = key
        q0, qn = span(key)
        rows = pl.ds(pl.multiple_of(sub * SUB, SUB), SUB)
        frows = pl.ds(pl.multiple_of(h * T + sub * SUB, SUB), SUB)
        k_tile = kv[d, h, 0, rows, :]
        s = dot(jnp.concatenate([k_tile, fk[d, frows, :]], axis=1), qt[:, q0:q0 + qn])
        if d == 0:
            key_pos = h * T + sub * SUB + lax.broadcasted_iota(jnp.int32, s.shape, 0)
            query_pos = q0 + lax.broadcasted_iota(jnp.int32, s.shape, 1)
            s = jnp.where(key_pos <= query_pos, s, -2.0 * MASK)
        return s, k_tile, kv[d, h, 1, rows, :]

    def forward(key):
        q0, qn = span(key)

        @pl.loop(0, T // SUB)
        def _(sub):
            s, _, v_tile = scores(key, sub)
            old = m_s[:, q0:q0 + qn]
            new = jnp.maximum(old, jnp.max(s, axis=0, keepdims=True))
            p = jnp.exp2((s - new) * LOG2)
            fade = jnp.exp2((old - new) * LOG2)
            m_s[:, q0:q0 + qn] = new
            l_s[:, q0:q0 + qn] = l_s[:, q0:q0 + qn] * fade + jnp.sum(p, axis=0, keepdims=True)
            ot[:, q0:q0 + qn] = ot[:, q0:q0 + qn] * fade + dot_tn(v_tile, p.astype(BF16))

    def grad_block(block):
        w_cols = w_in[:, pl.ds(pl.multiple_of(block * T, T), T)]
        for half in range(2):
            rows = slice(half * SUB, half * SUB + SUB)
            da[rows, :] = da[rows, :] + dot_nt(gmf[block, half], w_cols)

    def gm_step(k):
        step, half = k // 2 + 1, k % 2
        ring_recv(gmf, zg_s, zg_r, step, half)
        ring_send(gmf, zg_s, zg_r, step + 1, half)

    forward((0, 0))
    forward((0, 1))
    gm_step(0)
    kv_forward(4, 0)
    forward((4, 0))
    grad_block(z)
    gm_step(1)
    kv_forward(4, 1)
    kv_forward(1, 0)
    kv_forward(3, 0)
    forward((4, 1))
    forward((1, 0))

    @pl.loop(1, nz)
    def _(by):
        src = wsl.at[zed(-by), rows16, wide]
        remote(src, src, w1_s.at[by], w1_r.at[by], me, z).wait_recv()

    for by in range(1, NX):
        src = wsl.at[:, rows16, wide]
        start(remote(src, src, wx_s.at[by], wx_r.at[by], mate(0, by), z))
    gm_step(2)
    kv_forward(1, 1)
    kv_forward(3, 1)
    forward((1, 1))
    forward((3, 0))
    grad_block(zed(1))
    grad_block(zed(-1))
    gm_step(3)
    kv_recv(2, 0)
    forward((3, 1))
    forward((2, 0))
    for by in range(1, NX):
        src = wsl.at[:, pl.ds(pl.multiple_of((y * NX + lax.rem(x - by + NX, NX)) * 16, 16), 16), wide]
        remote(src, src, wx_s.at[by], wx_r.at[by], me, z).wait_recv()
    for by in range(1, ny):
        src = wsl.at[:, pl.ds(pl.multiple_of(y * NX * 16, 16), NX * 16), wide]
        start(remote(src, src, wy_s.at[by], wy_r.at[by], mate(by, 0), z))
    gm_step(4)
    kv_recv(2, 1)
    forward((2, 1))

    inv = 1.0 / l_s[...]
    lse = m_s[...] + jnp.log2(l_s[...]) * (1.0 / LOG2)
    att = ot[...] * inv
    otb[...] = att.astype(BF16)
    for h in range(2):
        ob[h] = att[:, h * T:(h + 1) * T].T.astype(BF16).reshape(2, SUB, HD)
    mine = cols(c, HD)
    start(remote(ob.at[o], atf.at[z, :, :, mine], at_s, at_r, sib, z))
    atf[z, :, :, mine] = ob[c]
    high, mid, low = thirds(lse)
    qt[HD:, :] = jnp.where(
        row == LSE_ROW, high,
        jnp.where(row == LSE_ROW + 1, mid, jnp.where(row == LSE_ROW + 2, low, qfeat)),
    ).astype(BF16)
    dst = atf.at[z, :, :, cols(o, HD)]
    remote(dst, dst, at_s, at_r, sib, z).wait_recv()

    order = (0, 1, -1, 2, -2, 3, -3, 4)
    per = nc // nz

    def weight_block(index):
        block = zed(order[index])
        part = dot_tn(atf[z, 0], gmf[block, 0]) + dot_tn(atf[z, 1], gmf[block, 1])
        pg[...] = part
        for e in range(per):
            gown[block * per + e] = pg[:, pl.ds(pl.multiple_of(e * SUB + c * HD, HD), HD)]
            gws[block * per + e] = pg[:, pl.ds(pl.multiple_of(e * SUB + o * HD, HD), HD)].astype(BF16)

    grad_block(zed(2))
    grad_block(zed(-2))
    gm_step(5)
    for half in range(2):
        ring_send(atf, za_s, za_r, 1, half)
    for index in range(5):
        weight_block(index)
    grad_block(zed(3))
    grad_block(zed(-3))
    gm_step(6)
    gm_step(7)
    grad_block(zed(4))

    dos[...] = da[:, cols(o, HD)].astype(BF16)
    start(remote(dos, dob.at[c], do_s, do_r, sib, z))
    dob[c] = da[:, mine].astype(BF16)
    for index in range(5, 8):
        weight_block(index)
    start(remote(gws, gwr, gx_s, gx_r, sib, z))

    remote(dob.at[o], dob.at[o], do_s, do_r, sib, z).wait_recv()
    dot_rows = jnp.concatenate([dob[0].astype(F32).T, dob[1].astype(F32).T], axis=1)
    dotr[:HD, :] = dot_rows.astype(BF16)
    delta = jnp.sum(dot_rows * otb[...].astype(F32), axis=0, keepdims=True)
    high, mid, low = thirds(delta)
    dotr[HD:, :] = jnp.where(
        row == 0, high, jnp.where(row == 1, mid, jnp.where(row == 2, low, 0.0))
    ).astype(BF16)
    dqt[...] = jnp.zeros(dqt.shape, F32)
    minus = jnp.where(lax.broadcasted_iota(jnp.int32, (SUB, HD), 1) < 3, -1.0, 0.0).astype(BF16)

    def backward(key, finish):
        q0, qn = span(key)

        @pl.loop(0, T // SUB)
        def _(sub):
            rows = pl.ds(pl.multiple_of(sub * SUB, SUB), SUB)
            s, k_tile, v_tile = scores(key, sub)
            p = jnp.exp2(s * LOG2)
            dp = dot(jnp.concatenate([v_tile, minus], axis=1), dotr[:, q0:q0 + qn])
            ds = (p * dp).astype(BF16)
            if qn == CT:
                do_rows = dob[...].reshape(CT, HD)
                q_rows = qs[...].reshape(CT, HD)
            else:
                do_rows = dob[q0 // T]
                q_rows = qs[q0 // T]
            finish(rows, dot(ds, q_rows) * SCALE, dot(p.astype(BF16), do_rows))
            dqt[:, q0:q0 + qn] = dqt[:, q0:q0 + qn] + dot_tn(k_tile, ds)

    def grads(slot, h):
        def finish(rows, dk, dv):
            acc[slot, h, 0, rows] = dk
            acc[slot, h, 1, rows] = dv

        backward((slot, h), finish)

    def gate(cond):
        return jnp.where(cond, 1.0, 0.0).astype(F32)

    side = jnp.where(x < 2, 0, 1)

    def back1(h):
        to = jnp.where(x < 2, mate(0, 1), mate(0, -1))
        return remote(snd.at[2, h], r1.at[side, h], c1_s.at[h], c1_r.at[side, h], to, z)

    def back1_add(h):
        for half in range(2):
            slot = 3 - 2 * half

            @pl.when(inner)
            def _():
                remote(r1.at[half, h], r1.at[half, h], c1_s.at[h], c1_r.at[half, h], me, z).wait_recv()
                snd[slot, h] = (acc[slot, h] + r1[half, h].astype(F32)).astype(BF16)

            @pl.when(jnp.logical_not(inner))
            def _():
                snd[slot, h] = acc[slot, h].astype(BF16)

        start(remote(snd.at[3, h], r2.at[0, h], c2_s.at[0, h], c2_r.at[0, h], mate(0, 1), z))
        start(remote(snd.at[1, h], r2.at[1, h], c2_s.at[1, h], c2_r.at[1, h], mate(0, -1), z))

    def back2_add(h):
        for half in range(2):
            remote(r2.at[half, h], r2.at[half, h], c2_s.at[half, h], c2_r.at[half, h], me, z).wait_recv()
        a, b = r2[0, h].astype(F32), r2[1, h].astype(F32)
        snd[REACH, h] = (acc[REACH, h] + a * gate(x > 0) + b * gate(x == NX - 1)).astype(BF16)
        start(remote(snd.at[REACH, h], r3.at[h], c3_s.at[h], c3_r.at[h], mate(-1, 0), z))
        acc[0, h] = acc[0, h] + a * gate(x == 0) + b * gate(x < NX - 1)

    def att_step(k):
        step, half = k // 2 + 1, k % 2
        ring_recv(atf, za_s, za_r, step, half)
        ring_send(atf, za_s, za_r, step + 1, half)

    for h in range(2):
        grads(2, h)
        snd[2, h] = acc[2, h].astype(BF16)
        start(back1(h))
    att_step(0)
    grads(1, 0)
    grads(3, 0)
    att_step(1)
    back1_add(0)
    grads(1, 1)
    att_step(2)
    grads(3, 1)
    back1_add(1)
    att_step(3)

    remote(gwr, gwr, gx_s, gx_r, sib, z).wait_recv()

    def row_of(by):
        return pl.ds(lax.rem(y + by, ny) * NX, NX)

    for by in range(1, ny):
        ysend[by] = (gown[row_of(by)] + gwr[row_of(by)].astype(F32)).astype(BF16)
        start(remote(ysend.at[by], yin.at[by], gy_s.at[by], gy_r.at[by], mate(by, 0), z))

    for by in range(1, ny):
        src = wsl.at[:, pl.ds(pl.multiple_of(lax.rem(y - by + ny, ny) * NX * 16, 16), NX * 16), wide]
        remote(src, src, wy_s.at[by], wy_r.at[by], me, z).wait_recv()
    start(remote(wsl.at[:, :, wide], wsl.at[:, :, wide], w3_s, w3_r, sib, z))

    grads(4, 0)
    att_step(4)
    grads(4, 1)
    grads(0, 0)
    att_step(5)
    grads(0, 1)
    back2_add(0)

    xown[...] = gown[row_of(0)] + gwr[row_of(0)].astype(F32)
    for by in range(1, ny):
        remote(yin.at[by], yin.at[by], gy_s.at[by], gy_r.at[by], me, z).wait_recv()
        xown[...] = xown[...] + yin[by].astype(F32)
    for by in range(1, NX):
        xsend[by] = xown[lax.rem(x + by, NX)].astype(BF16)
        start(remote(xsend.at[by], xin.at[by], gt_s.at[by], gt_r.at[by], mate(0, by), z))

    back2_add(1)

    fin[0, 0] = (dqt[:, :T] * SCALE).T.astype(BF16)
    fin[0, 1] = (dqt[:, T:] * SCALE).T.astype(BF16)
    outs = (dq_out, dk_out, dv_out)
    start(remote(fin.at[0, o], dq_out.at[:, mine], fn_s.at[0], fn_r.at[0], sib, z))
    dq_out[:, mine] = fin[0, c]

    other = wsl.at[:, :, cols(o, SUB)]
    remote(other, other, w3_s, w3_r, sib, z).wait_recv()

    def out_block(block, first=False):
        for half in range(2):
            rows = slice(half * SUB, half * SUB + SUB)
            part = dot(atf[block, half], wsl[block])
            lo[rows, :] = part if first else lo[rows, :] + part

    out_block(z, True)
    for by in (1, -1, 2, -2, 3, -3):
        out_block(zed(by))

    total = xown[x]
    for by in range(1, NX):
        remote(xin.at[by], xin.at[by], gt_s.at[by], gt_r.at[by], me, z).wait_recv()
        total = total + xin[by].astype(F32)
    gw_out[...] = total

    att_step(6)
    att_step(7)
    out_block(zed(4))
    out[...] = lo[...].astype(BF16)

    for h in range(2):
        remote(r3.at[h], r3.at[h], c3_s.at[h], c3_r.at[h], me, z).wait_recv()
        for t in range(2):
            fin[1 + t, h] = (acc[0, h, t] + r3[h, t].astype(F32)).astype(BF16)
    for t in (1, 2):
        start(remote(fin.at[t, o], outs[t].at[:, mine], fn_s.at[t], fn_r.at[t], sib, z))
        outs[t][:, mine] = fin[t, c]
    for t in range(3):
        dst = outs[t].at[:, cols(o, HD)]
        remote(dst, dst, fn_s.at[t], fn_r.at[t], sib, z).wait_recv()

    for copy in sent:
        copy.wait_send()

    @pl.loop(1, nz)
    def _(by):
        src = wsl.at[z, rows16, wide]
        remote(src, src, w1_s.at[by], w1_r.at[by], me, zed(by)).wait_send()

    for h in range(2):
        for slot in (1, 3, REACH):
            kv_copy(slot, h).wait_send()
        for half in range(2):
            pl.when(inner)(kv_on(half, h).wait_send)


def copy_kernel(*refs):
    for src, dst in zip(refs[:5], refs[5:]):
        dst[...] = src[...]


def body(nc, nz, queries, key_in, values, segment, tool_ids, out_weight, grad_mixed):
    width = out_weight.shape[1]
    vm = pltpu.VMEM
    dma = pltpu.SemaphoreType.DMA
    one = dma(())
    grads = (2, T, HD)
    scratch = [
        vm((2, T, HD), BF16),
        vm((REACH + 1, 2, 2, T, HD), BF16),
        vm((REACH + 1, CT, HD), BF16),
        vm((2 * HD, CT), BF16),
        vm((1, CT), F32), vm((1, CT), F32),
        vm((HD, CT), F32),
        vm((HD, CT), BF16),
        vm((2, 2, SUB, HD), BF16),
        vm((nz, 2, SUB, T), BF16),
        vm((T, 2 * HD), F32),
        vm((T, HD), BF16),
        vm((2, T, HD), BF16),
        vm((2 * HD, CT), BF16),
        vm((HD, CT), F32),
        vm((nz, 2 * HD, T), BF16),
        vm((nz, 2, SUB, 2 * HD), BF16),
        vm((T, T), F32),
        vm((REACH + 1, 2, *grads), F32),
        vm((REACH + 1, 2, *grads), BF16),
        vm((2, 2, *grads), BF16), vm((2, 2, *grads), BF16), vm((2, *grads), BF16),
        vm((3, 2, T, HD), BF16),
        vm((2 * HD, T), F32),
        vm((nc, 2 * HD, HD), F32),
        vm((nc, 2 * HD, HD), BF16), vm((nc, 2 * HD, HD), BF16),
        vm((nc // NX, NX, 2 * HD, HD), BF16), vm((nc // NX, NX, 2 * HD, HD), BF16),
        vm((NX, 2 * HD, HD), F32),
        vm((NX, 2 * HD, HD), BF16), vm((NX, 2 * HD, HD), BF16),
        dma((3,)), dma((3,)),
        dma((7, 2)), dma((REACH + 1, 2)),
        dma((16,)), dma((16,)), dma((16,)), dma((16,)),
        dma((nz,)), dma((nz,)),
        dma((NX,)), dma((NX,)), dma((nc // NX,)), dma((nc // NX,)), one, one,
        one, one, one, one,
        dma((2,)), dma((2, 2)), dma((2, 2)), dma((2, 2)), dma((2,)), dma((2,)),
        dma((3,)), dma((3,)), one, one,
        dma((nc // NX,)), dma((nc // NX,)), dma((NX,)), dma((NX,)),
    ]
    results = pl.pallas_call(
        functools.partial(kernel, nc, nz),
        out_shape=(
            jax.ShapeDtypeStruct((T, width // nz), BF16),
            jax.ShapeDtypeStruct(queries.shape, BF16),
            jax.ShapeDtypeStruct(queries.shape, BF16),
            jax.ShapeDtypeStruct(queries.shape, BF16),
            jax.ShapeDtypeStruct((2 * HD, width // (2 * nc)), F32),
        ),
        in_specs=[pl.BlockSpec(memory_space=pltpu.VMEM)] * 7,
        out_specs=[pl.BlockSpec(memory_space=pltpu.VMEM)] * 5,
        scratch_shapes=scratch,
        compiler_params=pltpu.CompilerParams(
            collective_id=0, has_side_effects=True, vmem_limit_bytes=58 * 1024 * 1024
        ),
        cost_estimate=pl.CostEstimate(
            flops=20_000_000_000, bytes_accessed=8_000_000, transcendentals=10_000_000
        ),
    )(
        segment.reshape(-1, HD), tool_ids.reshape(-1, HD),
        queries, key_in, values, out_weight, grad_mixed.reshape(2, SUB, width // nz),
    )
    return pl.pallas_call(
        copy_kernel,
        out_shape=tuple(jax.ShapeDtypeStruct(r.shape, r.dtype) for r in results),
        in_specs=[pl.BlockSpec(memory_space=pltpu.VMEM)] * 5,
        out_specs=[pl.BlockSpec(memory_space=pltpu.VMEM)] * 5,
    )(*results)


def solution(mesh):
    nc, nz = mesh.shape["ctx"] // 2, mesh.shape["head"]
    split = P("ctx", "head")
    return jax.shard_map(
        functools.partial(body, nc, nz),
        mesh=mesh,
        in_specs=(split, split, split, P(), P(), P("head", None), split),
        out_specs=(split, split, split, split, P("head", "ctx")),
        check_vma=False,
    )
```

```python
import functools
import math

import jax
import jax.numpy as jnp
from jax import lax
from jax.experimental import pallas as pl
from jax.experimental.pallas import tpu as pltpu
from jax.sharding import PartitionSpec as P

HD = 128
T = 512
CT = 1024
SUB = 256
NX = 4
REACH = 4
DOCS = 24
TOOLS = 16
LSE_ROW = DOCS + TOOLS
MASK = 131072.0
SCALE = 1.0 / math.sqrt(HD)
LOG2 = SCALE * math.log2(math.e)
MESH = pl.DeviceIdType.MESH
F32 = jnp.float32
BF16 = jnp.bfloat16


def dot(a, b):
    return jnp.dot(a, b, preferred_element_type=F32)


def dot_tn(a, b):
    return lax.dot_general(a, b, (((0,), (0,)), ((), ())), preferred_element_type=F32)


def dot_nt(a, b):
    return lax.dot_general(a, b, (((1,), (1,)), ((), ())), preferred_element_type=F32)


def thirds(x):
    high = x.astype(BF16)
    rest = x - high.astype(F32)
    mid = rest.astype(BF16)
    return high.astype(F32), mid.astype(F32), (rest - mid.astype(F32))


def kernel(
    nc, nz,
    seg, tool, q_in, k_in, v_in, w_hbm, gm_in,
    out, dq_out, dk_out, dv_out, gw_out,
    qw, kv, fk, qt, qtmp, m_s, l_s, ot, otb, ob, gmf, da, dos, dow, dot_t, dtmp, dqt, wsl, atf, lo, st,
    w_in, acc, fin, pg, gown, gws, gwr, ysend, yin, xown, xsend, xin,
    swap_s, swap_r, kv_s, kv_r, zg_s, zg_r, za_s, za_r, w1_s, w1_r, wx_s, wx_r, wy_s, wy_r,
    w3_s, w3_r, at_s, at_r, do_s, do_r, q_s, q_r, d_s, d_r, t_s, t_r,
    fn_s, fn_r, gx_s, gx_r, gy_s, gy_r, gt_s, gt_r, local_s,
):
    me = lax.axis_index("ctx")
    z = lax.axis_index("head")
    m = me // 2
    c = lax.rem(me, 2)
    o = 1 - c
    sib = me + 1 - 2 * c

    ny = nc // NX
    y = m // NX
    x = lax.rem(m, NX)

    def chip(by):
        return lax.rem(m + by + nc, nc)

    def mate(dy, dx):
        return 2 * (lax.rem(y + dy + ny, ny) * NX + lax.rem(x + dx + NX, NX)) + c

    def zed(by):
        return lax.rem(z + by + nz, nz)

    def remote(src, dst, ss, rs, ctx, head):
        return pltpu.make_async_remote_copy(
            src_ref=src, dst_ref=dst, send_sem=ss, recv_sem=rs,
            device_id=(ctx, head), device_id_type=MESH,
        )

    def cols(index, width):
        return pl.ds(pl.multiple_of(index * width, width), width)

    sent = []

    def start(copy):
        copy.start()
        sent.append(copy)

    local = [
        pltpu.make_async_copy(src, dst, local_s.at[index])
        for index, (src, dst) in enumerate((
            (w_hbm, w_in),
            (gm_in, gmf.at[z]),
            (q_in.at[:, :, cols(c, HD)], qw.at[0, :, c]),
            (k_in.at[:, cols(c, HD)], kv.at[0, c, 0]),
            (v_in.at[:, cols(c, HD)], kv.at[0, c, 1]),
        ))
    ]
    for copy in local:
        copy.start()

    barrier = pltpu.get_barrier_semaphore()
    pl.semaphore_signal(barrier, inc=1, device_id=(sib, z), device_id_type=MESH)

    for by in range(1, NX):
        pl.semaphore_signal(barrier, inc=1, device_id=(mate(0, by), z), device_id_type=MESH)
    for by in range(1, ny):
        pl.semaphore_signal(barrier, inc=1, device_id=(mate(by, 0), z), device_id_type=MESH)

    @pl.loop(1, nz)
    def _(by):
        pl.semaphore_signal(barrier, inc=1, device_id=(me, zed(by)), device_id_type=MESH)

    pl.semaphore_wait(barrier, 1 + (NX - 1) + (ny - 1) + (nz - 1))

    swaps = (
        (q_in.at[:, :, cols(o, HD)], qw.at[0, :, c], qw.at[0, :, o]),
        (k_in.at[:, cols(o, HD)], kv.at[0, c, 0], kv.at[0, o, 0]),
        (v_in.at[:, cols(o, HD)], kv.at[0, c, 1], kv.at[0, o, 1]),
    )
    for t, (src, dst, _) in enumerate(swaps):
        start(remote(src, dst, swap_s.at[t], swap_r.at[t], sib, z))

    full = nz // 2 - 1

    def ring_has(step, part, parts, right):
        return step <= full or (step == full + 1 and (part * 2 < parts) == right)

    def ring_send(buf, ss, rs, step, part, parts, src=None):
        for side, right in enumerate((True, False)):
            if ring_has(step, part, parts, right):
                block = zed(1 - step) if right else zed(step - 1)
                to = zed(1) if right else zed(-1)
                k = (side * (full + 1) + step - 1) * parts + part
                dst = buf.at[block, part]
                start(remote(dst if src is None else src, dst, ss.at[k], rs.at[k], me, to))

    def ring_recv(buf, ss, rs, step, part, parts):
        for side, right in enumerate((True, False)):
            if ring_has(step, part, parts, right):
                block = zed(-step) if right else zed(step)
                k = (side * (full + 1) + step - 1) * parts + part
                dst = buf.at[block, part]
                remote(dst, dst, ss.at[k], rs.at[k], me, z).wait_recv()

    def gm_send(j):
        for part in (2 * j, 2 * j + 1):
            ring_send(gmf, zg_s, zg_r, 1, part, 4, gm_in.at[part])

    def gm_step(j, step):
        for part in (2 * j, 2 * j + 1):
            ring_recv(gmf, zg_s, zg_r, step, part, 4)
            ring_send(gmf, zg_s, zg_r, step + 1, part, 4)

    gm_send(0)

    for copy in local:
        copy.wait()

    rows16 = pl.ds(pl.multiple_of(m * 16, 16), 16)
    wide = cols(c, SUB)

    @pl.loop(1, nz)
    def _(by):
        to = zed(by)
        src = w_in.at[rows16, pl.ds(pl.multiple_of(to * T + c * SUB, SUB), SUB)]
        remote(src, wsl.at[z, rows16, wide], w1_s.at[by], w1_r.at[by], me, to).start()

    wsl[z, rows16, wide] = w_in[rows16, pl.ds(pl.multiple_of(z * T + c * SUB, SUB), SUB)]

    for t, (_, _, dst) in enumerate(swaps):
        remote(dst, dst, swap_s.at[t], swap_r.at[t], sib, z).wait_recv()

    inner = (x == 1) | (x == 2)

    class Tree:
        def __init__(self, buf, ss, rs, sign):
            self.refs = buf, ss, rs
            self.sign = sign
            self.at = x if sign > 0 else NX - 1 - x

        def copy(self, slot, i):
            buf, ss, rs = self.refs
            if slot == 1:
                src, to = jnp.where(self.at < NX - 1, 0, REACH), mate(0, self.sign)
            elif slot == 3:
                src, to = jnp.where(self.at > 0, REACH, 0), mate(0, -self.sign)
            else:
                src, to = 0, mate(self.sign, 0)
            return remote(buf.at[src, i], buf.at[slot, i], ss.at[slot, i], rs.at[slot, i], to, z)

        def on(self, slot, i):
            buf, ss, rs = self.refs
            to = mate(0, self.sign if slot == 1 else -self.sign)
            return remote(buf.at[slot, i], buf.at[2, i], ss.at[5 + slot // 2, i], rs.at[2, i], to, z)

        def first(self, i):
            pl.when(self.at < NX - 1)(self.copy(1, i).start)
            pl.when(self.at == 0)(self.copy(3, i).start)
            self.copy(REACH, i).start()

        def take(self, slot, i):
            buf, ss, rs = self.refs
            remote(buf.at[slot, i], buf.at[slot, i], ss.at[slot, i], rs.at[slot, i], me, z).wait_recv()
            if slot == REACH:
                pl.when(self.at == NX - 1)(self.copy(1, i).start)
                pl.when(self.at > 0)(self.copy(3, i).start)
            elif slot != 2:
                pl.when(inner)(self.on(slot, i).start)

        def drain(self):
            for i in range(2):
                for slot in (1, 3, REACH):
                    self.copy(slot, i).wait_send()
                for slot in (1, 3):
                    pl.when(inner)(self.on(slot, i).wait_send)

    kvs = Tree(kv, kv_s, kv_r, 1)
    qts = Tree(qw, q_s, q_r, -1)
    dts = Tree(dow, d_s, d_r, -1)
    sts = Tree(st, t_s, t_r, -1)
    for i in range(2):
        kvs.first(i)

    def ids(ref, index, order=(0, 1, 2, 3, 4, 5, 6, 7)):
        rows = ref[pl.ds(pl.multiple_of(index * 8, 8), 8), :]
        return jnp.concatenate([rows[r:r + 1, :] for r in order], axis=1)

    row = lax.broadcasted_iota(jnp.int32, (HD, CT), 0)
    pos = lax.broadcasted_iota(jnp.int32, (HD, CT), 1)
    block64 = lax.shift_right_logical(pos, 6)
    is_doc = row < DOCS
    is_tool = (row >= DOCS) & (row < LSE_ROW)
    for d in range(REACH + 2):
        back = -d if d <= REACH else 0
        seg_row, tool_row = ids(seg, chip(back)), ids(tool, chip(back))
        if d == 0:
            bad_tool = (block64 > row - DOCS) | ((tool_row != 0) & (block64 != row - DOCS))
        else:
            bad_tool = jnp.broadcast_to(tool_row != 0, row.shape)
        bad = (is_doc & (seg_row != row)) | (is_tool & bad_tool)
        feat = jnp.where(bad, -MASK, jnp.where((row >= LSE_ROW) & (row < LSE_ROW + 3), -1.0, 0.0))
        fk[d] = feat.T.astype(BF16)

    half_row = lax.broadcasted_iota(jnp.int32, (HD, T), 0)
    half_pos = lax.broadcasted_iota(jnp.int32, (HD, T), 1)

    def query_features(d, j):
        q = (0, 1, 4, 5) if j == 0 else (2, 3, 6, 7)
        seg_row = ids(seg, chip(d), q)
        here = lax.shift_right_logical(half_pos, 8) * 8 + j * 4 + lax.shift_right_logical(half_pos & (SUB - 1), 6)
        hot = ((half_row < DOCS) & (seg_row == half_row)) | (
            (half_row >= DOCS) & (half_row < LSE_ROW) & (here == half_row - DOCS)
        )
        return jnp.where(hot, 1.0, 0.0)

    def with_lse(feat, stats):
        high, mid, low = thirds(stats)
        return jnp.where(
            half_row == LSE_ROW, high,
            jnp.where(half_row == LSE_ROW + 1, mid, jnp.where(half_row == LSE_ROW + 2, low, feat)),
        ).astype(BF16)

    def with_delta(stats):
        high, mid, low = thirds(stats)
        return jnp.where(
            half_row == 0, high, jnp.where(half_row == 1, mid, jnp.where(half_row == 2, low, 0.0))
        ).astype(BF16)

    for j in range(2):
        qt[j, :HD, :] = qw[0, j].reshape(T, HD).astype(F32).T.astype(BF16)
        qt[j, HD:, :] = query_features(0, j).astype(BF16)
    m_s[...] = jnp.full(m_s.shape, -1e30, F32)
    l_s[...] = jnp.zeros(l_s.shape, F32)
    ot[...] = jnp.zeros(ot.shape, F32)
    da[...] = jnp.zeros(da.shape, F32)

    def scores(qtr, d, h, start_row, count, features, own, first=0):
        rows = pl.ds(start_row, count)
        frows = pl.ds(h * T + start_row, count)
        k_tile = kv[d, h, 0, rows, :]
        s = dot(jnp.concatenate([k_tile, fk[features, frows, :]], axis=1), qtr)
        if own is not None:
            key_pos = h * T + start_row + lax.broadcasted_iota(jnp.int32, s.shape, 0)
            q = first + lax.broadcasted_iota(jnp.int32, s.shape, 1)
            query_pos = lax.shift_right_logical(q, 8) * T + own * SUB + (q & (SUB - 1))
            s = jnp.where(key_pos <= query_pos, s, -2.0 * MASK)
        return s, k_tile, kv[d, h, 1, rows, :]

    def spans(d, h):
        if (d, h) == (0, 1):
            return SUB, SUB
        if (d, h) == (REACH, 0):
            return 0, SUB
        return 0, T

    def forward(key):
        d, h = key
        q0, qn = spans(d, h)

        for j in range(2):
            qsl = slice(q0, q0 + qn)
            s, _, v_tile = scores(qt[j, :, qsl], d, h, 0, T, d, j if d == 0 else None, q0)
            old = m_s[j, :, qsl]
            new = jnp.maximum(old, jnp.max(s, axis=0, keepdims=True))
            p = jnp.exp2((s - new) * LOG2)
            fade = jnp.exp2((old - new) * LOG2)
            m_s[j, :, qsl] = new
            l_s[j, :, qsl] = l_s[j, :, qsl] * fade + jnp.sum(p, axis=0, keepdims=True)
            ot[j, :, qsl] = ot[j, :, qsl] * fade + dot_tn(v_tile, p.astype(BF16))

    order = (0, 1, -1, 2, -2, 3, -3, 4)

    def grad_blocks(j, indices):
        for index in indices:
            block = zed(order[index])
            w_cols = w_in[:, pl.ds(pl.multiple_of(block * T, T), T)]
            da[j] = da[j] + dot_nt(gmf[block, 2 * j:2 * j + 2].reshape(SUB, T), w_cols)

    mine = cols(c, HD)

    def grad_out(j):
        dos[j] = da[j, :, cols(o, HD)].astype(BF16)
        start(remote(dos.at[j], dow.at[0, j, c], do_s.at[j], do_r.at[j], sib, z))
        dow[0, j, c] = da[j, :, mine].astype(BF16)

    def grad_in(j):
        dst = dow.at[0, j, o]
        remote(dst, dst, do_s.at[j], do_r.at[j], sib, z).wait_recv()
        dts.first(j)

    def stats(j):
        rows = dow[0, j].reshape(T, HD).astype(F32).T
        dot_t[j, :HD, :] = rows.astype(BF16)
        st[0, j, 1:2, :] = jnp.sum(rows * otb[j].astype(F32), axis=0, keepdims=True)
        dot_t[j, HD:, :] = with_delta(st[0, j, 1:2, :])
        sts.first(j)

    def parts(qtr, dtr, d, h, features, own=None, first=0):
        s, k_tile, v_tile = scores(qtr, d, h, 0, T, features, own, first)
        p = jnp.exp2(s * LOG2)
        minus = jnp.where(lax.broadcasted_iota(jnp.int32, (T, HD), 1) < 3, -1.0, 0.0).astype(BF16)
        ds = p * dot(jnp.concatenate([v_tile, minus], axis=1), dtr)
        return k_tile, p.astype(BF16), ds.astype(BF16)

    def add_keys(h, p, ds, q_rows, do_rows):
        acc[h, 0] = acc[h, 0] + dot(ds, q_rows)
        acc[h, 1] = acc[h, 1] + dot(p, do_rows)

    def grad_query(j, d, h):
        q0, qn = spans(d, h)
        qsl = slice(q0, q0 + qn)
        own = j if d == 0 else None
        k_tile, p, ds = parts(qt[j, :, qsl], dot_t[j, :, qsl], d, h, d, own, q0)
        dqt[j, :, qsl] = dqt[j, :, qsl] + dot_tn(k_tile, ds)
        if d == 0:
            add_keys(h, p, ds, qw[0, j].reshape(T, HD)[q0:q0 + qn], dow[0, j].reshape(T, HD)[q0:q0 + qn])

    def grad_keys(j, d):
        qtmp[:HD, :] = qw[d, j].reshape(T, HD).astype(F32).T.astype(BF16)
        qtmp[HD:, :] = with_lse(query_features(d, j), st[d, j, 0:1, :])
        dtmp[:HD, :] = dow[d, j].reshape(T, HD).astype(F32).T.astype(BF16)
        dtmp[HD:, :] = with_delta(st[d, j, 1:2, :])
        for h in range(2):
            q0, qn = spans(d, h)
            _, p, ds = parts(qtmp[:, q0:q0 + qn], dtmp[:, q0:q0 + qn], 0, h, REACH + 1)
            add_keys(h, p, ds, qw[d, j].reshape(T, HD)[q0:q0 + qn], dow[d, j].reshape(T, HD)[q0:q0 + qn])

    def att_step(k):
        step, part = k // 2 + 1, k % 2
        ring_recv(atf, za_s, za_r, step, part, 2)
        ring_send(atf, za_s, za_r, step + 1, part, 2)

    per = nc // nz

    def weight_block(index):
        block = zed(order[index])
        pg[...] = dot_tn(atf[z, 0], gmf[block, 0:2].reshape(SUB, T)) + dot_tn(
            atf[z, 1], gmf[block, 2:4].reshape(SUB, T)
        )
        for e in range(per):
            gown[block * per + e] = pg[:, pl.ds(pl.multiple_of(e * SUB + c * HD, HD), HD)]
            gws[block * per + e] = pg[:, pl.ds(pl.multiple_of(e * SUB + o * HD, HD), HD)].astype(BF16)
        pair = pl.ds(block * per, per)
        start(remote(gws.at[pair], gwr.at[pair], gx_s.at[index], gx_r.at[index], sib, z))

    forward((0, 0))
    gm_step(0, 1)
    kvs.take(4, 0)
    forward((0, 1))
    gm_step(0, 2)
    kvs.take(4, 1)
    forward((4, 0))
    kvs.take(1, 0)
    kvs.take(3, 0)
    forward((4, 1))
    gm_step(0, 3)
    gm_send(1)
    kvs.take(1, 1)
    kvs.take(3, 1)
    forward((1, 0))
    grad_blocks(0, (0, 1, 2))
    gm_step(0, 4)
    grad_blocks(0, (3, 4, 5, 6, 7))
    grad_out(0)
    forward((3, 0))
    kvs.take(2, 0)
    for i in range(2):
        qts.first(i)

    @pl.loop(1, nz)
    def _(by):
        src = wsl.at[zed(-by), rows16, wide]
        remote(src, src, w1_s.at[by], w1_r.at[by], me, z).wait_recv()

    for by in range(1, NX):
        src = wsl.at[:, rows16, wide]
        start(remote(src, src, wx_s.at[by], wx_r.at[by], mate(0, by), z))
    gm_step(1, 1)
    grad_in(0)
    forward((1, 1))
    forward((3, 1))
    kvs.take(2, 1)
    qts.take(4, 0)
    qts.take(4, 1)
    gm_step(1, 2)
    forward((2, 0))
    forward((2, 1))

    for j in range(2):
        att = ot[j] * (1.0 / l_s[j])
        otb[j] = att.astype(BF16)
        st[0, j] = jnp.broadcast_to(m_s[j] + jnp.log2(l_s[j]) * (1.0 / LOG2), (8, T))
        for h in range(2):
            ob[h, j] = att[:, h * SUB:(h + 1) * SUB].T.astype(BF16)
    start(remote(ob.at[o], atf.at[z, :, :, mine], at_s, at_r, sib, z))
    stats(0)
    dts.take(4, 0)
    atf[z, :, :, mine] = ob[c]
    for j in range(2):
        qt[j, HD:, :] = with_lse(query_features(0, j), st[0, j, 0:1, :])
    for by in range(1, NX):
        src = wsl.at[:, pl.ds(pl.multiple_of((y * NX + lax.rem(x - by + NX, NX)) * 16, 16), 16), wide]
        remote(src, src, wx_s.at[by], wx_r.at[by], me, z).wait_recv()
    for by in range(1, ny):
        src = wsl.at[:, pl.ds(pl.multiple_of(y * NX * 16, 16), NX * 16), wide]
        start(remote(src, src, wy_s.at[by], wy_r.at[by], mate(by, 0), z))
    dqt[...] = jnp.zeros(dqt.shape, F32)
    acc[...] = jnp.zeros(acc.shape, F32)
    dst = atf.at[z, :, :, cols(o, HD)]
    remote(dst, dst, at_s, at_r, sib, z).wait_recv()
    gm_step(1, 3)
    for half in range(2):
        ring_send(atf, za_s, za_r, 1, half, 2)
    for i in range(2):
        qts.take(1, i)
        qts.take(3, i)
    dts.take(1, 0)
    dts.take(3, 0)
    sts.take(4, 0)
    grad_blocks(1, (0, 1, 2, 3, 4, 5, 6))
    for index in range(7):
        weight_block(index)
    grad_query(0, 0, 0)
    grad_query(0, 0, 1)
    for h in range(2):
        grad_query(0, 1, h)
        grad_query(0, 2, h)
    gm_step(1, 4)
    grad_blocks(1, (7,))
    grad_out(1)
    weight_block(7)
    sts.take(1, 0)
    sts.take(3, 0)
    att_step(0)
    grad_in(1)
    stats(1)
    for index in range(8):
        pair = pl.ds(zed(order[index]) * per, per)
        remote(gwr.at[pair], gwr.at[pair], gx_s.at[index], gx_r.at[index], sib, z).wait_recv()

    def row_of(by):
        return pl.ds(lax.rem(y + by, ny) * NX, NX)

    for by in range(1, ny):
        ysend[by] = (gown[row_of(by)] + gwr[row_of(by)].astype(F32)).astype(BF16)
        start(remote(ysend.at[by], yin.at[by], gy_s.at[by], gy_r.at[by], mate(by, 0), z))
    grad_keys(0, 4)
    att_step(1)
    for i in range(2):
        qts.take(2, i)
    dts.take(2, 0)
    sts.take(2, 0)
    for h in range(2):
        grad_query(0, 3, h)
    dts.take(4, 1)
    sts.take(4, 1)
    for h in range(2):
        grad_query(0, 4, h)
    att_step(2)
    grad_keys(0, 1)
    grad_keys(0, 3)
    for slot in (1, 3):
        dts.take(slot, 1)
        sts.take(slot, 1)
    att_step(3)

    for by in range(1, ny):
        src = wsl.at[:, pl.ds(pl.multiple_of(lax.rem(y - by + ny, ny) * NX * 16, 16), NX * 16), wide]
        remote(src, src, wy_s.at[by], wy_r.at[by], me, z).wait_recv()
    start(remote(wsl.at[:, :, wide], wsl.at[:, :, wide], w3_s, w3_r, sib, z))
    for h in range(2):
        grad_query(1, 0, h)
    for h in range(2):
        grad_query(1, 1, h)
    att_step(4)
    grad_keys(0, 2)
    for h in range(2):
        grad_query(1, 2, h)
    att_step(5)
    dts.take(2, 1)
    sts.take(2, 1)

    xown[...] = gown[row_of(0)] + gwr[row_of(0)].astype(F32)
    for by in range(1, ny):
        remote(yin.at[by], yin.at[by], gy_s.at[by], gy_r.at[by], me, z).wait_recv()
        xown[...] = xown[...] + yin[by].astype(F32)
    for by in range(1, NX):
        xsend[by] = xown[lax.rem(x + by, NX)].astype(BF16)
        start(remote(xsend.at[by], xin.at[by], gt_s.at[by], gt_r.at[by], mate(0, by), z))
    for d in (4, 1, 3, 2):
        grad_keys(1, d)

    outs = (dq_out, dk_out, dv_out)
    for h in range(2):
        fin[1, h] = (acc[h, 0] * SCALE).astype(BF16)
        fin[2, h] = acc[h, 1].astype(BF16)
    for t in (1, 2):
        start(remote(fin.at[t, o], outs[t].at[:, mine], fn_s.at[t], fn_r.at[t], sib, z))
        outs[t][:, mine] = fin[t, c]

    for d in (3, 4):
        for h in range(2):
            grad_query(1, d, h)
    for h in range(2):
        for j in range(2):
            fin[0, h, j * SUB:(j + 1) * SUB] = (dqt[j, :, h * SUB:(h + 1) * SUB] * SCALE).T.astype(BF16)
    start(remote(fin.at[0, o], dq_out.at[:, mine], fn_s.at[0], fn_r.at[0], sib, z))
    dq_out[:, mine] = fin[0, c]

    other = wsl.at[:, :, cols(o, SUB)]
    remote(other, other, w3_s, w3_r, sib, z).wait_recv()

    def out_block(block, first=False):
        for half in range(2):
            rows = slice(half * SUB, half * SUB + SUB)
            part = dot(atf[block, half], wsl[block])
            lo[rows, :] = part if first else lo[rows, :] + part

    out_block(z, True)
    for by in (1, -1, 2, -2, 3, -3):
        out_block(zed(by))

    total = xown[x]
    for by in range(1, NX):
        remote(xin.at[by], xin.at[by], gt_s.at[by], gt_r.at[by], me, z).wait_recv()
        total = total + xin[by].astype(F32)
    gw_out[...] = total

    att_step(6)
    att_step(7)
    out_block(zed(4))
    out[...] = lo[...].astype(BF16)
    for t in range(3):
        dst = outs[t].at[:, cols(o, HD)]
        remote(dst, dst, fn_s.at[t], fn_r.at[t], sib, z).wait_recv()

    for copy in sent:
        copy.wait_send()

    @pl.loop(1, nz)
    def _(by):
        src = wsl.at[z, rows16, wide]
        remote(src, src, w1_s.at[by], w1_r.at[by], me, zed(by)).wait_send()

    for tree in (kvs, qts, dts, sts):
        tree.drain()


def copy_kernel(*refs):
    for src, dst in zip(refs[:5], refs[5:]):
        dst[...] = src[...]


def body(nc, nz, queries, key_in, values, segment, tool_ids, out_weight, grad_mixed):
    width = out_weight.shape[1]
    vm = pltpu.VMEM
    dma = pltpu.SemaphoreType.DMA
    one = dma(())
    grads = (2, T, HD)
    halves = (2, 2, SUB, HD)
    scratch = [
        vm((REACH + 1, *halves), BF16),
        vm((REACH + 1, 2, 2, T, HD), BF16),
        vm((REACH + 2, CT, HD), BF16),
        vm((2, 2 * HD, T), BF16), vm((2 * HD, T), BF16),
        vm((2, 1, T), F32), vm((2, 1, T), F32),
        vm((2, HD, T), F32),
        vm((2, HD, T), BF16),
        vm(halves, BF16),
        vm((nz, 4, HD, T), BF16),
        vm((2, SUB, 2 * HD), F32),
        vm((2, SUB, HD), BF16),
        vm((REACH + 1, *halves), BF16),
        vm((2, 2 * HD, T), BF16), vm((2 * HD, T), BF16),
        vm((2, HD, T), F32),
        vm((nz, 2 * HD, T), BF16),
        vm((nz, 2, SUB, 2 * HD), BF16),
        vm((T, T), F32),
        vm((REACH + 1, 2, 8, T), F32),
        vm((2 * HD, width), BF16),
        vm((2, *grads), F32),
        vm((3, 2, T, HD), BF16),
        vm((2 * HD, T), F32),
        vm((nc, 2 * HD, HD), F32),
        vm((nc, 2 * HD, HD), BF16), vm((nc, 2 * HD, HD), BF16),
        vm((nc // NX, NX, 2 * HD, HD), BF16), vm((nc // NX, NX, 2 * HD, HD), BF16),
        vm((NX, 2 * HD, HD), F32),
        vm((NX, 2 * HD, HD), BF16), vm((NX, 2 * HD, HD), BF16),
        dma((3,)), dma((3,)),
        dma((7, 2)), dma((REACH + 1, 2)),
        dma((4 * nz,)), dma((4 * nz,)), dma((2 * nz,)), dma((2 * nz,)),
        dma((nz,)), dma((nz,)),
        dma((NX,)), dma((NX,)), dma((nc // NX,)), dma((nc // NX,)), one, one,
        one, one, dma((2,)), dma((2,)),
        dma((7, 2)), dma((REACH + 1, 2)),
        dma((7, 2)), dma((REACH + 1, 2)),
        dma((7, 2)), dma((REACH + 1, 2)),
        dma((3,)), dma((3,)), dma((nz,)), dma((nz,)),
        dma((nc // NX,)), dma((nc // NX,)), dma((NX,)), dma((NX,)), dma((5,)),
    ]
    results = pl.pallas_call(
        functools.partial(kernel, nc, nz),
        out_shape=(
            jax.ShapeDtypeStruct((T, width // nz), BF16),
            jax.ShapeDtypeStruct(queries.shape, BF16),
            jax.ShapeDtypeStruct(queries.shape, BF16),
            jax.ShapeDtypeStruct(queries.shape, BF16),
            jax.ShapeDtypeStruct((2 * HD, width // (2 * nc)), F32),
        ),
        in_specs=[pl.BlockSpec(memory_space=pltpu.VMEM)] * 2 + [pl.BlockSpec(memory_space=pl.ANY)] * 5,
        out_specs=[pl.BlockSpec(memory_space=pltpu.VMEM)] * 5,
        scratch_shapes=scratch,
        compiler_params=pltpu.CompilerParams(
            collective_id=0, has_side_effects=True, vmem_limit_bytes=58 * 1024 * 1024
        ),
        cost_estimate=pl.CostEstimate(
            flops=20_000_000_000, bytes_accessed=8_000_000, transcendentals=10_000_000
        ),
    )(
        segment.reshape(-1, HD), tool_ids.reshape(-1, HD),
        queries.reshape(2, SUB, 2 * HD), key_in, values, out_weight, grad_mixed.reshape(4, HD, width // nz),
    )
    return pl.pallas_call(
        copy_kernel,
        out_shape=tuple(jax.ShapeDtypeStruct(r.shape, r.dtype) for r in results),
        in_specs=[pl.BlockSpec(memory_space=pltpu.VMEM)] * 5,
        out_specs=[pl.BlockSpec(memory_space=pltpu.VMEM)] * 5,
    )(*results)


def solution(mesh):
    nc, nz = mesh.shape["ctx"] // 2, mesh.shape["head"]
    split = P("ctx", "head")
    return jax.shard_map(
        functools.partial(body, nc, nz),
        mesh=mesh,
        in_specs=(split, split, split, P(), P(), P("head", None), split),
        out_specs=(split, split, split, split, P("head", "ctx")),
        check_vma=False,
    )
```

```python
import functools
import math

import jax
import jax.numpy as jnp
from jax import lax
from jax.experimental import pallas as pl
from jax.experimental.pallas import tpu as pltpu
from jax.sharding import PartitionSpec as P

HD = 128
T = 512
CT = 1024
SUB = 256
NX = 4
REACH = 4
DOCS = 24
TOOLS = 16
LSE_ROW = DOCS + TOOLS
MASK = 131072.0
SCALE = 1.0 / math.sqrt(HD)
LOG2 = SCALE * math.log2(math.e)
MESH = pl.DeviceIdType.MESH
F32 = jnp.float32
BF16 = jnp.bfloat16


def dot(a, b):
    return jnp.dot(a, b, preferred_element_type=F32)


def dot_tn(a, b):
    return lax.dot_general(a, b, (((0,), (0,)), ((), ())), preferred_element_type=F32)


def dot_nt(a, b):
    return lax.dot_general(a, b, (((1,), (1,)), ((), ())), preferred_element_type=F32)


def thirds(x):
    high = x.astype(BF16)
    rest = x - high.astype(F32)
    mid = rest.astype(BF16)
    return high.astype(F32), mid.astype(F32), (rest - mid.astype(F32))


def kernel(
    nc, nz,
    seg, tool, q_in, k_in, v_in, w_hbm, gm_in,
    out, dq_out, dk_out, dv_out, gw_out,
    qw, kv, fk, qt, qtmp, m_s, l_s, ot, otb, ob, gmf, da, dos, dow, dot_t, dtmp, dqt, wsl, atf, lo, st,
    w_in, acc, fin, pg, gown, gws, gwr, ysend, yin, xown, xsend, xin,
    swap_s, swap_r, kv_s, kv_r, zg_s, zg_r, za_s, za_r, w1_s, w1_r, wx_s, wx_r, wy_s, wy_r,
    w3_s, w3_r, at_s, at_r, do_s, do_r, q_s, q_r, d_s, d_r, t_s, t_r,
    fn_s, fn_r, gx_s, gx_r, gy_s, gy_r, gt_s, gt_r, local_s,
):
    me = lax.axis_index("ctx")
    z = lax.axis_index("head")
    m = me // 2
    c = lax.rem(me, 2)
    o = 1 - c
    sib = me + 1 - 2 * c

    ny = nc // NX
    y = m // NX
    x = lax.rem(m, NX)

    def chip(by):
        return lax.rem(m + by + nc, nc)

    def mate(dy, dx):
        return 2 * (lax.rem(y + dy + ny, ny) * NX + lax.rem(x + dx + NX, NX)) + c

    def zed(by):
        return lax.rem(z + by + nz, nz)

    def remote(src, dst, ss, rs, ctx, head):
        return pltpu.make_async_remote_copy(
            src_ref=src, dst_ref=dst, send_sem=ss, recv_sem=rs,
            device_id=(ctx, head), device_id_type=MESH,
        )

    def cols(index, width):
        return pl.ds(pl.multiple_of(index * width, width), width)

    sent = []

    def start(copy):
        copy.start()
        sent.append(copy)

    local = [
        pltpu.make_async_copy(src, dst, local_s.at[index])
        for index, (src, dst) in enumerate((
            (w_hbm, w_in),
            (gm_in, gmf.at[z]),
            (q_in.at[:, :, cols(c, HD)], qw.at[0, :, c]),
            (k_in.at[:, cols(c, HD)], kv.at[0, c, 0]),
            (v_in.at[:, cols(c, HD)], kv.at[0, c, 1]),
        ))
    ]
    for copy in local:
        copy.start()

    barrier = pltpu.get_barrier_semaphore()
    pl.semaphore_signal(barrier, inc=1, device_id=(sib, z), device_id_type=MESH)

    for by in range(1, NX):
        pl.semaphore_signal(barrier, inc=1, device_id=(mate(0, by), z), device_id_type=MESH)
    for by in range(1, ny):
        pl.semaphore_signal(barrier, inc=1, device_id=(mate(by, 0), z), device_id_type=MESH)

    @pl.loop(1, nz)
    def _(by):
        pl.semaphore_signal(barrier, inc=1, device_id=(me, zed(by)), device_id_type=MESH)

    pl.semaphore_wait(barrier, 1 + (NX - 1) + (ny - 1) + (nz - 1))

    swaps = (
        (q_in.at[:, :, cols(o, HD)], qw.at[0, :, c], qw.at[0, :, o]),
        (k_in.at[:, cols(o, HD)], kv.at[0, c, 0], kv.at[0, o, 0]),
        (v_in.at[:, cols(o, HD)], kv.at[0, c, 1], kv.at[0, o, 1]),
    )
    for t, (src, dst, _) in enumerate(swaps):
        start(remote(src, dst, swap_s.at[t], swap_r.at[t], sib, z))

    full = nz // 2 - 1

    def ring_has(step, part, parts, right):
        return step <= full or (step == full + 1 and (part * 2 < parts) == right)

    def ring_send(buf, ss, rs, step, part, parts, src=None):
        for side, right in enumerate((True, False)):
            if ring_has(step, part, parts, right):
                block = zed(1 - step) if right else zed(step - 1)
                to = zed(1) if right else zed(-1)
                k = (side * (full + 1) + step - 1) * parts + part
                dst = buf.at[block, part]
                start(remote(dst if src is None else src, dst, ss.at[k], rs.at[k], me, to))

    def ring_recv(buf, ss, rs, step, part, parts):
        for side, right in enumerate((True, False)):
            if ring_has(step, part, parts, right):
                block = zed(-step) if right else zed(step)
                k = (side * (full + 1) + step - 1) * parts + part
                dst = buf.at[block, part]
                remote(dst, dst, ss.at[k], rs.at[k], me, z).wait_recv()

    def gm_send(j):
        for part in (2 * j, 2 * j + 1):
            ring_send(gmf, zg_s, zg_r, 1, part, 4, gm_in.at[part])

    def gm_step(j, step):
        for part in (2 * j, 2 * j + 1):
            ring_recv(gmf, zg_s, zg_r, step, part, 4)
            ring_send(gmf, zg_s, zg_r, step + 1, part, 4)

    gm_send(0)

    for copy in local:
        copy.wait()

    rows16 = pl.ds(pl.multiple_of(m * 16, 16), 16)
    wide = cols(c, SUB)

    @pl.loop(1, nz)
    def _(by):
        to = zed(by)
        src = w_in.at[rows16, pl.ds(pl.multiple_of(to * T + c * SUB, SUB), SUB)]
        remote(src, wsl.at[z, rows16, wide], w1_s.at[by], w1_r.at[by], me, to).start()

    wsl[z, rows16, wide] = w_in[rows16, pl.ds(pl.multiple_of(z * T + c * SUB, SUB), SUB)]

    for t, (_, _, dst) in enumerate(swaps):
        remote(dst, dst, swap_s.at[t], swap_r.at[t], sib, z).wait_recv()

    inner = (x == 1) | (x == 2)

    class Tree:
        def __init__(self, buf, ss, rs, sign):
            self.refs = buf, ss, rs
            self.sign = sign
            self.at = x if sign > 0 else NX - 1 - x

        def copy(self, slot, i):
            buf, ss, rs = self.refs
            if slot == 1:
                src, to = jnp.where(self.at < NX - 1, 0, REACH), mate(0, self.sign)
            elif slot == 3:
                src, to = jnp.where(self.at > 0, REACH, 0), mate(0, -self.sign)
            else:
                src, to = 0, mate(self.sign, 0)
            return remote(buf.at[src, i], buf.at[slot, i], ss.at[slot, i], rs.at[slot, i], to, z)

        def on(self, slot, i):
            buf, ss, rs = self.refs
            to = mate(0, self.sign if slot == 1 else -self.sign)
            return remote(buf.at[slot, i], buf.at[2, i], ss.at[5 + slot // 2, i], rs.at[2, i], to, z)

        def first(self, i):
            pl.when(self.at < NX - 1)(self.copy(1, i).start)
            pl.when(self.at == 0)(self.copy(3, i).start)
            self.copy(REACH, i).start()

        def take(self, slot, i):
            buf, ss, rs = self.refs
            remote(buf.at[slot, i], buf.at[slot, i], ss.at[slot, i], rs.at[slot, i], me, z).wait_recv()
            if slot == REACH:
                pl.when(self.at == NX - 1)(self.copy(1, i).start)
                pl.when(self.at > 0)(self.copy(3, i).start)
            elif slot != 2:
                pl.when(inner)(self.on(slot, i).start)

        def drain(self):
            for i in range(2):
                for slot in (1, 3, REACH):
                    self.copy(slot, i).wait_send()
                for slot in (1, 3):
                    pl.when(inner)(self.on(slot, i).wait_send)

    kvs = Tree(kv, kv_s, kv_r, 1)
    qts = Tree(qw, q_s, q_r, -1)
    dts = Tree(dow, d_s, d_r, -1)
    sts = Tree(st, t_s, t_r, -1)
    for i in range(2):
        kvs.first(i)

    def ids(ref, index, order=(0, 1, 2, 3, 4, 5, 6, 7)):
        rows = ref[pl.ds(pl.multiple_of(index * 8, 8), 8), :]
        return jnp.concatenate([rows[r:r + 1, :] for r in order], axis=1)

    row = lax.broadcasted_iota(jnp.int32, (HD, CT), 0)
    pos = lax.broadcasted_iota(jnp.int32, (HD, CT), 1)
    block64 = lax.shift_right_logical(pos, 6)
    is_doc = row < DOCS
    is_tool = (row >= DOCS) & (row < LSE_ROW)
    for d in range(REACH + 2):
        back = -d if d <= REACH else 0
        seg_row, tool_row = ids(seg, chip(back)), ids(tool, chip(back))
        if d == 0:
            bad_tool = (block64 > row - DOCS) | ((tool_row != 0) & (block64 != row - DOCS))
        else:
            bad_tool = jnp.broadcast_to(tool_row != 0, row.shape)
        bad = (is_doc & (seg_row != row)) | (is_tool & bad_tool)
        feat = jnp.where(bad, -MASK, jnp.where((row >= LSE_ROW) & (row < LSE_ROW + 3), -1.0, 0.0))
        fk[d] = feat.T.astype(BF16)

    half_row = lax.broadcasted_iota(jnp.int32, (HD, T), 0)
    half_pos = lax.broadcasted_iota(jnp.int32, (HD, T), 1)

    def query_features(d, j):
        q = (0, 1, 4, 5) if j == 0 else (2, 3, 6, 7)
        seg_row = ids(seg, chip(d), q)
        here = lax.shift_right_logical(half_pos, 8) * 8 + j * 4 + lax.shift_right_logical(half_pos & (SUB - 1), 6)
        hot = ((half_row < DOCS) & (seg_row == half_row)) | (
            (half_row >= DOCS) & (half_row < LSE_ROW) & (here == half_row - DOCS)
        )
        return jnp.where(hot, 1.0, 0.0)

    def with_lse(feat, stats):
        high, mid, low = thirds(stats)
        return jnp.where(
            half_row == LSE_ROW, high,
            jnp.where(half_row == LSE_ROW + 1, mid, jnp.where(half_row == LSE_ROW + 2, low, feat)),
        ).astype(BF16)

    def with_delta(stats):
        high, mid, low = thirds(stats)
        return jnp.where(
            half_row == 0, high, jnp.where(half_row == 1, mid, jnp.where(half_row == 2, low, 0.0))
        ).astype(BF16)

    for j in range(2):
        qt[j, :HD, :] = qw[0, j].reshape(T, HD).astype(F32).T.astype(BF16)
        qt[j, HD:, :] = query_features(0, j).astype(BF16)
    m_s[...] = jnp.full(m_s.shape, -1e30, F32)
    l_s[...] = jnp.zeros(l_s.shape, F32)
    ot[...] = jnp.zeros(ot.shape, F32)
    da[...] = jnp.zeros(da.shape, F32)

    def scores(qtr, d, h, start_row, count, features, own, first=0):
        rows = pl.ds(start_row, count)
        frows = pl.ds(h * T + start_row, count)
        k_tile = kv[d, h, 0, rows, :]
        s = dot(jnp.concatenate([k_tile, fk[features, frows, :]], axis=1), qtr)
        if own is not None:
            key_pos = h * T + start_row + lax.broadcasted_iota(jnp.int32, s.shape, 0)
            q = first + lax.broadcasted_iota(jnp.int32, s.shape, 1)
            query_pos = lax.shift_right_logical(q, 8) * T + own * SUB + (q & (SUB - 1))
            s = jnp.where(key_pos <= query_pos, s, -2.0 * MASK)
        return s, k_tile, kv[d, h, 1, rows, :]

    def spans(d, h):
        if (d, h) == (0, 1):
            return SUB, SUB
        if (d, h) == (REACH, 0):
            return 0, SUB
        return 0, T

    def forward(key):
        d, h = key
        q0, qn = spans(d, h)

        for j in range(2):
            qsl = slice(q0, q0 + qn)
            s, _, v_tile = scores(qt[j, :, qsl], d, h, 0, T, d, j if d == 0 else None, q0)
            old = m_s[j, :, qsl]
            new = jnp.maximum(old, jnp.max(s, axis=0, keepdims=True))
            p = jnp.exp2((s - new) * LOG2)
            fade = jnp.exp2((old - new) * LOG2)
            m_s[j, :, qsl] = new
            l_s[j, :, qsl] = l_s[j, :, qsl] * fade + jnp.sum(p, axis=0, keepdims=True)
            ot[j, :, qsl] = ot[j, :, qsl] * fade + dot_tn(v_tile, p.astype(BF16))

    order = (0, 1, -1, 2, -2, 3, -3, 4)

    def grad_blocks(j, indices):
        for index in indices:
            block = zed(order[index])
            w_cols = w_in[:, pl.ds(pl.multiple_of(block * T, T), T)]
            da[j] = da[j] + dot_nt(gmf[block, 2 * j:2 * j + 2].reshape(SUB, T), w_cols)

    mine = cols(c, HD)

    def grad_out(j):
        dos[j] = da[j, :, cols(o, HD)].astype(BF16)
        start(remote(dos.at[j], dow.at[0, j, c], do_s.at[j], do_r.at[j], sib, z))
        dow[0, j, c] = da[j, :, mine].astype(BF16)

    def grad_in(j):
        dst = dow.at[0, j, o]
        remote(dst, dst, do_s.at[j], do_r.at[j], sib, z).wait_recv()
        dts.first(j)

    def stats(j):
        rows = dow[0, j].reshape(T, HD).astype(F32).T
        dot_t[j, :HD, :] = rows.astype(BF16)
        st[0, j, 1:2, :] = jnp.sum(rows * otb[j].astype(F32), axis=0, keepdims=True)
        dot_t[j, HD:, :] = with_delta(st[0, j, 1:2, :])
        sts.first(j)

    def parts(qtr, dtr, d, h, features, own=None, first=0):
        s, k_tile, v_tile = scores(qtr, d, h, 0, T, features, own, first)
        p = jnp.exp2(s * LOG2)
        minus = jnp.where(lax.broadcasted_iota(jnp.int32, (T, HD), 1) < 3, -1.0, 0.0).astype(BF16)
        ds = p * dot(jnp.concatenate([v_tile, minus], axis=1), dtr)
        return k_tile, p.astype(BF16), ds.astype(BF16)

    def add_keys(h, p, ds, q_rows, do_rows):
        acc[h, 0] = acc[h, 0] + dot(ds, q_rows)
        acc[h, 1] = acc[h, 1] + dot(p, do_rows)

    def grad_query(j, d, h):
        q0, qn = spans(d, h)
        qsl = slice(q0, q0 + qn)
        own = j if d == 0 else None
        k_tile, p, ds = parts(qt[j, :, qsl], dot_t[j, :, qsl], d, h, d, own, q0)
        dqt[j, :, qsl] = dqt[j, :, qsl] + dot_tn(k_tile, ds)
        if d == 0:
            add_keys(h, p, ds, qw[0, j].reshape(T, HD)[q0:q0 + qn], dow[0, j].reshape(T, HD)[q0:q0 + qn])

    def grad_keys(j, d):
        qtmp[:HD, :] = qw[d, j].reshape(T, HD).astype(F32).T.astype(BF16)
        qtmp[HD:, :] = with_lse(query_features(d, j), st[d, j, 0:1, :])
        dtmp[:HD, :] = dow[d, j].reshape(T, HD).astype(F32).T.astype(BF16)
        dtmp[HD:, :] = with_delta(st[d, j, 1:2, :])
        for h in range(2):
            q0, qn = spans(d, h)
            _, p, ds = parts(qtmp[:, q0:q0 + qn], dtmp[:, q0:q0 + qn], 0, h, REACH + 1)
            add_keys(h, p, ds, qw[d, j].reshape(T, HD)[q0:q0 + qn], dow[d, j].reshape(T, HD)[q0:q0 + qn])

    def att_step(k):
        step, part = k // 2 + 1, k % 2
        ring_recv(atf, za_s, za_r, step, part, 2)
        ring_send(atf, za_s, za_r, step + 1, part, 2)

    per = nc // nz

    def weight_block(index):
        block = zed(order[index])
        pg[...] = dot_tn(atf[z, 0], gmf[block, 0:2].reshape(SUB, T)) + dot_tn(
            atf[z, 1], gmf[block, 2:4].reshape(SUB, T)
        )
        for e in range(per):
            gown[block * per + e] = pg[:, pl.ds(pl.multiple_of(e * SUB + c * HD, HD), HD)]
            gws[block * per + e] = pg[:, pl.ds(pl.multiple_of(e * SUB + o * HD, HD), HD)].astype(BF16)
        pair = pl.ds(block * per, per)
        start(remote(gws.at[pair], gwr.at[pair], gx_s.at[index], gx_r.at[index], sib, z))

    forward((0, 0))
    gm_step(0, 1)
    kvs.take(4, 0)
    forward((0, 1))
    gm_step(0, 2)
    kvs.take(4, 1)
    forward((4, 0))
    kvs.take(1, 0)
    kvs.take(3, 0)
    forward((4, 1))
    gm_step(0, 3)
    gm_send(1)
    kvs.take(1, 1)
    kvs.take(3, 1)
    forward((1, 0))
    grad_blocks(0, (0, 1, 2))
    gm_step(0, 4)
    grad_blocks(0, (3, 4, 5, 6, 7))
    grad_out(0)
    forward((3, 0))
    kvs.take(2, 0)
    for i in range(2):
        qts.first(i)

    @pl.loop(1, nz)
    def _(by):
        src = wsl.at[zed(-by), rows16, wide]
        remote(src, src, w1_s.at[by], w1_r.at[by], me, z).wait_recv()

    for by in range(1, NX):
        src = wsl.at[:, rows16, wide]
        start(remote(src, src, wx_s.at[by], wx_r.at[by], mate(0, by), z))
    gm_step(1, 1)
    grad_in(0)
    forward((1, 1))
    forward((3, 1))
    kvs.take(2, 1)
    qts.take(4, 0)
    qts.take(4, 1)
    gm_step(1, 2)
    forward((2, 0))
    forward((2, 1))

    for j in range(2):
        att = ot[j] * (1.0 / l_s[j])
        otb[j] = att.astype(BF16)
        st[0, j] = jnp.broadcast_to(m_s[j] + jnp.log2(l_s[j]) * (1.0 / LOG2), (8, T))
        for h in range(2):
            ob[h, j] = att[:, h * SUB:(h + 1) * SUB].T.astype(BF16)
    start(remote(ob.at[o], atf.at[z, :, :, mine], at_s, at_r, sib, z))
    stats(0)
    dts.take(4, 0)
    atf[z, :, :, mine] = ob[c]
    for j in range(2):
        qt[j, HD:, :] = with_lse(query_features(0, j), st[0, j, 0:1, :])
    for by in range(1, NX):
        src = wsl.at[:, pl.ds(pl.multiple_of((y * NX + lax.rem(x - by + NX, NX)) * 16, 16), 16), wide]
        remote(src, src, wx_s.at[by], wx_r.at[by], me, z).wait_recv()
    def w_rows(by):
        return pl.ds(pl.multiple_of(lax.rem(y + by + ny, ny) * NX * 16, 16), NX * 16)

    def w_copy(way, on):
        if on:
            src = wsl.at[pl.ds(way * (nz // 2), nz // 2), w_rows(2 * way - 1), wide]
        else:
            src = wsl.at[:, w_rows(0), wide]
        return remote(src, src, wy_s.at[way, on], wy_r.at[way, on], mate(1 - 2 * way, 0), z)

    def w_take(way, on):
        if on:
            dst = wsl.at[pl.ds(way * (nz // 2), nz // 2), w_rows(2), wide]
        else:
            dst = wsl.at[:, w_rows(2 * way - 1), wide]
        remote(dst, dst, wy_s.at[way, on], wy_r.at[way, on], me, z).wait_recv()

    for way in range(2):
        start(w_copy(way, 0))
    dqt[...] = jnp.zeros(dqt.shape, F32)
    acc[...] = jnp.zeros(acc.shape, F32)
    dst = atf.at[z, :, :, cols(o, HD)]
    remote(dst, dst, at_s, at_r, sib, z).wait_recv()
    gm_step(1, 3)
    for half in range(2):
        ring_send(atf, za_s, za_r, 1, half, 2)
    for i in range(2):
        qts.take(1, i)
        qts.take(3, i)
    dts.take(1, 0)
    dts.take(3, 0)
    sts.take(4, 0)
    grad_blocks(1, (0, 1, 2, 3, 4, 5, 6))
    for index in range(7):
        weight_block(index)
    grad_query(0, 0, 0)
    grad_query(0, 0, 1)
    for h in range(2):
        grad_query(0, 1, h)
        grad_query(0, 2, h)
    gm_step(1, 4)
    grad_blocks(1, (7,))
    grad_out(1)
    weight_block(7)
    sts.take(1, 0)
    sts.take(3, 0)
    att_step(0)
    grad_in(1)
    stats(1)
    for index in range(8):
        pair = pl.ds(zed(order[index]) * per, per)
        remote(gwr.at[pair], gwr.at[pair], gx_s.at[index], gx_r.at[index], sib, z).wait_recv()

    def pieces(by, half):
        return pl.ds(lax.rem(y + by, ny) * NX + half * (NX // 2), NX // 2)

    def share(by, half):
        rows = pieces(by, half)
        return gown[rows] + gwr[rows].astype(F32)

    def y_copy(way, message):
        to = mate(1 - 2 * way, 0)
        return remote(
            ysend.at[way, message], yin.at[way, message], gy_s.at[way, message], gy_r.at[way, message], to, z
        )

    def y_take(way, message):
        y_copy(way, message).wait_recv()
        return yin[way, message].astype(F32)

    for way in range(2):
        ysend[way, 0] = share(2, way).astype(BF16)
        start(y_copy(way, 0))
    for way in range(2):
        ysend[way, 1] = share(1 + 2 * way, 1 - way).astype(BF16)
        start(y_copy(way, 1))
    grad_keys(0, 4)
    att_step(1)
    for i in range(2):
        qts.take(2, i)
    dts.take(2, 0)
    sts.take(2, 0)
    for way in range(2):
        w_take(way, 0)
        start(w_copy(way, 1))
    for h in range(2):
        grad_query(0, 3, h)
    dts.take(4, 1)
    sts.take(4, 1)
    for h in range(2):
        grad_query(0, 4, h)
    att_step(2)
    grad_keys(0, 1)
    for way in range(2):
        ysend[way, 2] = (share(1 + 2 * way, way) + y_take(way, 0)).astype(BF16)
        start(y_copy(way, 2))
    grad_keys(0, 3)
    for slot in (1, 3):
        dts.take(slot, 1)
        sts.take(slot, 1)
    att_step(3)

    for way in range(2):
        w_take(way, 1)
    start(remote(wsl.at[:, :, wide], wsl.at[:, :, wide], w3_s, w3_r, sib, z))
    for h in range(2):
        grad_query(1, 0, h)
    for h in range(2):
        grad_query(1, 1, h)
    att_step(4)
    grad_keys(0, 2)
    for h in range(2):
        grad_query(1, 2, h)
    att_step(5)
    dts.take(2, 1)
    sts.take(2, 1)

    for half in range(2):
        xown[half * 2:half * 2 + 2] = share(0, half) + y_take(half, 2) + y_take(1 - half, 1)
    for by in range(1, NX):
        xsend[by] = xown[lax.rem(x + by, NX)].astype(BF16)
        start(remote(xsend.at[by], xin.at[by], gt_s.at[by], gt_r.at[by], mate(0, by), z))
    for d in (4, 1, 3, 2):
        grad_keys(1, d)

    outs = (dq_out, dk_out, dv_out)
    for h in range(2):
        fin[1, h] = (acc[h, 0] * SCALE).astype(BF16)
        fin[2, h] = acc[h, 1].astype(BF16)
    for t in (1, 2):
        start(remote(fin.at[t, o], outs[t].at[:, mine], fn_s.at[t], fn_r.at[t], sib, z))
        outs[t][:, mine] = fin[t, c]

    for d in (3, 4):
        for h in range(2):
            grad_query(1, d, h)
    for h in range(2):
        for j in range(2):
            fin[0, h, j * SUB:(j + 1) * SUB] = (dqt[j, :, h * SUB:(h + 1) * SUB] * SCALE).T.astype(BF16)
    start(remote(fin.at[0, o], dq_out.at[:, mine], fn_s.at[0], fn_r.at[0], sib, z))
    dq_out[:, mine] = fin[0, c]

    other = wsl.at[:, :, cols(o, SUB)]
    remote(other, other, w3_s, w3_r, sib, z).wait_recv()

    def out_block(block, first=False):
        for half in range(2):
            rows = slice(half * SUB, half * SUB + SUB)
            part = dot(atf[block, half], wsl[block])
            lo[rows, :] = part if first else lo[rows, :] + part

    out_block(z, True)
    for by in (1, -1, 2, -2, 3, -3):
        out_block(zed(by))

    total = xown[x]
    for by in range(1, NX):
        remote(xin.at[by], xin.at[by], gt_s.at[by], gt_r.at[by], me, z).wait_recv()
        total = total + xin[by].astype(F32)
    gw_out[...] = total

    att_step(6)
    att_step(7)
    out_block(zed(4))
    out[...] = lo[...].astype(BF16)
    for t in range(3):
        dst = outs[t].at[:, cols(o, HD)]
        remote(dst, dst, fn_s.at[t], fn_r.at[t], sib, z).wait_recv()

    for copy in sent:
        copy.wait_send()

    @pl.loop(1, nz)
    def _(by):
        src = wsl.at[z, rows16, wide]
        remote(src, src, w1_s.at[by], w1_r.at[by], me, zed(by)).wait_send()

    for tree in (kvs, qts, dts, sts):
        tree.drain()


def copy_kernel(*refs):
    for src, dst in zip(refs[:5], refs[5:]):
        dst[...] = src[...]


def body(nc, nz, queries, key_in, values, segment, tool_ids, out_weight, grad_mixed):
    width = out_weight.shape[1]
    vm = pltpu.VMEM
    dma = pltpu.SemaphoreType.DMA
    one = dma(())
    grads = (2, T, HD)
    halves = (2, 2, SUB, HD)
    scratch = [
        vm((REACH + 1, *halves), BF16),
        vm((REACH + 1, 2, 2, T, HD), BF16),
        vm((REACH + 2, CT, HD), BF16),
        vm((2, 2 * HD, T), BF16), vm((2 * HD, T), BF16),
        vm((2, 1, T), F32), vm((2, 1, T), F32),
        vm((2, HD, T), F32),
        vm((2, HD, T), BF16),
        vm(halves, BF16),
        vm((nz, 4, HD, T), BF16),
        vm((2, SUB, 2 * HD), F32),
        vm((2, SUB, HD), BF16),
        vm((REACH + 1, *halves), BF16),
        vm((2, 2 * HD, T), BF16), vm((2 * HD, T), BF16),
        vm((2, HD, T), F32),
        vm((nz, 2 * HD, T), BF16),
        vm((nz, 2, SUB, 2 * HD), BF16),
        vm((T, T), F32),
        vm((REACH + 1, 2, 8, T), F32),
        vm((2 * HD, width), BF16),
        vm((2, *grads), F32),
        vm((3, 2, T, HD), BF16),
        vm((2 * HD, T), F32),
        vm((nc, 2 * HD, HD), F32),
        vm((nc, 2 * HD, HD), BF16), vm((nc, 2 * HD, HD), BF16),
        vm((2, 3, NX // 2, 2 * HD, HD), BF16), vm((2, 3, NX // 2, 2 * HD, HD), BF16),
        vm((NX, 2 * HD, HD), F32),
        vm((NX, 2 * HD, HD), BF16), vm((NX, 2 * HD, HD), BF16),
        dma((3,)), dma((3,)),
        dma((7, 2)), dma((REACH + 1, 2)),
        dma((4 * nz,)), dma((4 * nz,)), dma((2 * nz,)), dma((2 * nz,)),
        dma((nz,)), dma((nz,)),
        dma((NX,)), dma((NX,)), dma((2, 2)), dma((2, 2)), one, one,
        one, one, dma((2,)), dma((2,)),
        dma((7, 2)), dma((REACH + 1, 2)),
        dma((7, 2)), dma((REACH + 1, 2)),
        dma((7, 2)), dma((REACH + 1, 2)),
        dma((3,)), dma((3,)), dma((nz,)), dma((nz,)),
        dma((2, 3)), dma((2, 3)), dma((NX,)), dma((NX,)), dma((5,)),
    ]
    results = pl.pallas_call(
        functools.partial(kernel, nc, nz),
        out_shape=(
            jax.ShapeDtypeStruct((T, width // nz), BF16),
            jax.ShapeDtypeStruct(queries.shape, BF16),
            jax.ShapeDtypeStruct(queries.shape, BF16),
            jax.ShapeDtypeStruct(queries.shape, BF16),
            jax.ShapeDtypeStruct((2 * HD, width // (2 * nc)), F32),
        ),
        in_specs=[pl.BlockSpec(memory_space=pltpu.VMEM)] * 2 + [pl.BlockSpec(memory_space=pl.ANY)] * 5,
        out_specs=[pl.BlockSpec(memory_space=pltpu.VMEM)] * 5,
        scratch_shapes=scratch,
        compiler_params=pltpu.CompilerParams(
            collective_id=0, has_side_effects=True, vmem_limit_bytes=58 * 1024 * 1024
        ),
        cost_estimate=pl.CostEstimate(
            flops=20_000_000_000, bytes_accessed=8_000_000, transcendentals=10_000_000
        ),
    )(
        segment.reshape(-1, HD), tool_ids.reshape(-1, HD),
        queries.reshape(2, SUB, 2 * HD), key_in, values, out_weight, grad_mixed.reshape(4, HD, width // nz),
    )
    return pl.pallas_call(
        copy_kernel,
        out_shape=tuple(jax.ShapeDtypeStruct(r.shape, r.dtype) for r in results),
        in_specs=[pl.BlockSpec(memory_space=pltpu.VMEM)] * 5,
        out_specs=[pl.BlockSpec(memory_space=pltpu.VMEM)] * 5,
    )(*results)


def solution(mesh):
    nc, nz = mesh.shape["ctx"] // 2, mesh.shape["head"]
    split = P("ctx", "head")
    return jax.shard_map(
        functools.partial(body, nc, nz),
        mesh=mesh,
        in_specs=(split, split, split, P(), P(), P("head", None), split),
        out_specs=(split, split, split, split, P("head", "ctx")),
        check_vma=False,
    )
```
